32 devices in a mesh: seq: 32 (over z, y, x, core).
Axes of the slice: x: 2, y: 2, z: 4, core: 2. Of those that a mesh axis runs over, the one named last changes fastest.
Arguments:
- acceptance_gate: bfloat16 [4096, 2048], P('seq'), may hold values from -1.1953125 to 1.1953125
- lookup_matrix: bfloat16 [4096, 2048], P('seq'), may hold values from -0.29882812 to 0.29882812
- payload_matrix: bfloat16 [4096, 2048], P('seq'), may hold values from -6 to 6
- fading_parameter: float32 [4096, 2048], P('seq'), may hold values from -17 to 0.5
- present_reward: float32 [2048], replicated, may hold values from -4 to 4
- emitted_cotangent: bfloat16 [4096, 2048], P('seq'), may hold values from -0.119628906 to 0.119628906
- paper_spans: int32 [64], replicated, may hold values from 1 to 1024, 4096 in all
Outputs:
- grad_receptance: bfloat16 [4096, 2048], P('seq')
- grad_key: bfloat16 [4096, 2048], P('seq')
- grad_value: bfloat16 [4096, 2048], P('seq')
- grad_decay: bfloat16 [4096, 2048], P('seq')
- reward_cotangent: float32 [2048], replicated
The draws below stay inside these ranges and needn't reach their ends.
Inputs may be any that keep to these rules, and one draw needn't show every extreme that they name: `paper_spans`: the 64 documents fill the packed sequence of 4096 tokens in order.
All inputs are finite; a program needn't handle non-finite values.
Results may differ from the reference program's by a relative error of at most 0.001.
Values sent between devices are 32-bit elements; how exact they have to be, the bound alone decides.
A program may use at most 320 MiB of HBM per device.

```python
import math
import jax
import jax.numpy as jnp
import numpy as np
from jax import lax

HEADS = 32
HS = 64
BL = 128
TOK_DEV = 128
FEATURE_DIM = 2048
TOKENS = 4096
NDOCS = 64


def draw_fading_parameter(key, part):
    keys = jax.random.split(jax.random.fold_in(key, 17), 7)
    share = 0.5
    quick = jax.random.uniform(keys[0], (HEADS, 1)) < share
    fast_rate = jnp.exp(jax.random.uniform(keys[1], (HEADS, HS), jnp.float32, math.log(math.log(10.0) / 50.0), math.log(math.log(10.0) / 30.0)))
    slow_rate = jnp.exp(jax.random.uniform(keys[2], (HEADS, HS), jnp.float32, math.log(math.log(10.0) / (40.0 * TOKENS)), math.log(math.log(10.0) / (4.0 * TOKENS))))
    starting_displacement = jnp.where(quick, fast_rate, slow_rate).reshape(1, FEATURE_DIM)
    splitting_multiplier = jnp.exp(jax.random.uniform(keys[3], (TOKENS // TOK_DEV, 1, FEATURE_DIM), jnp.float32, -math.log(2.0), math.log(2.0)))
    splitting_multiplier = jnp.broadcast_to(splitting_multiplier, (TOKENS // TOK_DEV, TOK_DEV, FEATURE_DIM)).reshape(TOKENS, FEATURE_DIM)
    approximate_guess = jnp.exp(jax.random.uniform(keys[4], (TOKENS, FEATURE_DIM), jnp.float32, -math.log(2.0), math.log(2.0)))
    arrangement_sequence = jax.random.randint(keys[5], (3,), 0, TOKENS)
    displacement_offsets = jax.random.uniform(keys[6], (3,), jnp.float32, 0.22, 0.69)
    symbol_total = jnp.arange(TOKENS)
    cluster_batch = jnp.sum(jnp.where(symbol_total[:, None] == arrangement_sequence[None, :], displacement_offsets[None, :], 0.0), axis=1)
    fading_speed = starting_displacement * splitting_multiplier * approximate_guess + cluster_batch[:, None]
    return jnp.log(fading_speed).astype(jnp.float32)


def block_scale(rng, shape, shards, smallest, top_value):
    factor_of, own = 1.0, jax.random.fold_in(rng, 6)
    for dim, shards_of in shards:
        draws = jnp.exp(jax.random.uniform(jax.random.fold_in(own, dim), (shards_of,), jnp.float32, smallest / len(shards), top_value / len(shards)))
        factor_of = factor_of * jnp.repeat(draws, shape[dim] // shards_of).reshape([-1 if axis == dim else 1 for axis in range(len(shape))])
    return factor_of


def split_up(count, total, most, lean):
    loads = [(1 << 20) // math.isqrt(rank ** lean) + 1 for rank in range(2, count + 1)]
    spare, counts = total - most - (count - 1), [1] * (count - 1)
    while spare > 0:
        free = [i for i in range(count - 1) if counts[i] < most]
        pool, budget = sum([loads[i] for i in free]), spare
        for i in free:
            more = min(most - counts[i], max(1, budget * loads[i] // pool), spare)
            counts[i] = counts[i] + more
            spare = spare - more
    return np.array([most] + counts)


def ragged(rng, amount, total, limit, skew):
    if amount == 2:
        one = jax.random.randint(rng, (), max(1, total - limit), min(limit, total - 1) + 1)
        return jnp.stack([one, total - one])
    tallies = jnp.asarray(split_up(amount, total, limit, skew), jnp.int32)
    pairs = (amount - 1) // 2
    source_of, taker = tallies[1:1 + 2 * pairs:2], tallies[2:2 + 2 * pairs:2]
    margin = jnp.minimum(source_of - 1, limit - taker)
    shifted = jax.random.randint(jax.random.fold_in(rng, 1), (pairs,), 0, 1 << 20) % (margin + 1)
    tallies = tallies.at[1:1 + 2 * pairs:2].set(source_of - shifted).at[2:2 + 2 * pairs:2].set(taker + shifted)
    return tallies[jax.random.permutation(jax.random.fold_in(rng, 2), amount)]


def centred(stream_key, dims, deviation, most, shards=(), held_as=jnp.bfloat16):
    result = deviation * jax.random.normal(stream_key, dims, jnp.float32)
    if shards:
        result = result * block_scale(stream_key, dims, shards, -0.22, 0.18)
    return jnp.clip(result, -most, most).astype(held_as)


def setup_inputs(seed: int = 0) -> dict:
    splits = jax.random.split(jax.random.key(seed), 8)
    return {
        "acceptance_gate": centred(splits[0], (TOKENS, FEATURE_DIM), 0.2, 1.1953125, ((0, 32),)),
        "lookup_matrix": centred(splits[1], (TOKENS, FEATURE_DIM), 0.05, 0.29882812, ((0, 32),)),
        "payload_matrix": centred(splits[2], (TOKENS, FEATURE_DIM), 1.0, 6.0, ((0, 32),)),
        "fading_parameter": draw_fading_parameter(jax.random.fold_in(splits[7], 71), 0),
        "present_reward": centred(splits[4], (FEATURE_DIM,), 1.0, 4.0, (), jnp.float32),
        "emitted_cotangent": centred(splits[5], (TOKENS, FEATURE_DIM), 0.02, 0.119628906, ((0, 32),)),
        "paper_spans": ragged(splits[6], NDOCS, TOKENS, TOKENS // 4, 2).astype(jnp.int32),
    }


def tile_advance_update(acceptance_line_tile, lookup_line_tile, payload_line_tile, source_line_tile, reward_array, portion_number, prior_memory, evolving_memory):
    element_total, width = acceptance_line_tile.shape
    attention_heads_total, tile_length = (evolving_memory.shape[0], evolving_memory.shape[1])
    hp = lax.Precision.HIGHEST
    logw = -jnp.exp(source_line_tile)
    cum = jnp.cumsum(logw, axis=0)
    before = cum - logw
    carried = (portion_number == prior_memory).astype(jnp.float32)
    query = (acceptance_line_tile * jnp.exp(before)).reshape(element_total, attention_heads_total, tile_length)
    keyed = (lookup_line_tile * jnp.exp(-cum)).reshape(element_total, attention_heads_total, tile_length)
    values = payload_line_tile.reshape(element_total, attention_heads_total, tile_length)
    scores = jnp.einsum('jhi,shi->hjs', query, keyed, precision=hp)
    arrangement_sequence = jnp.arange(element_total)
    allowed = (arrangement_sequence[:, None] > arrangement_sequence[None, :]) & (portion_number[:, None] == portion_number[None, :])
    scores = jnp.where(allowed[None], scores, 0.0)
    concluding_answer = jnp.einsum('hjs,shc->jhc', scores, values, precision=hp)
    concluding_answer = concluding_answer + carried[:, None, None] * jnp.einsum('jhi,hic->jhc', query, evolving_memory, precision=hp)
    immediate_contribution = lax.optimization_barrier(jnp.sum((acceptance_line_tile * reward_array[None, :] * lookup_line_tile).reshape(element_total, attention_heads_total, tile_length), axis=2))
    concluding_answer = concluding_answer + immediate_contribution[:, :, None] * values
    keep = (portion_number == portion_number[-1]).astype(jnp.float32)
    ending = (lookup_line_tile * jnp.exp(cum[-1][None, :] - cum) * keep[:, None]).reshape(element_total, attention_heads_total, tile_length)
    through = jnp.exp(cum[-1]) * (portion_number[-1] == prior_memory).astype(jnp.float32)
    fresh = through.reshape(attention_heads_total, tile_length)[:, :, None] * evolving_memory + jnp.einsum('shi,shc->hic', ending, values, precision=hp)
    return (concluding_answer.reshape(element_total, width), fresh)

def reference(acceptance_gate, lookup_matrix, payload_matrix, fading_parameter, present_reward, emitted_cotangent, paper_spans):
    starts = (jnp.cumsum(paper_spans) - paper_spans).astype(jnp.int32)
    positions = jnp.arange(TOKENS, dtype=jnp.int32)
    portion_number = (lax.optimization_barrier(jnp.sum((starts[None, :] <= positions[:, None]).astype(jnp.int32), axis=1)) - 1).astype(jnp.int32)
    prevs = jnp.concatenate([jnp.full((1,), -1, jnp.int32), portion_number[:-1]]).astype(jnp.int32)
    nblocks = TOKENS // BL
    seg_blocks = portion_number.reshape(nblocks, BL)
    prev_blocks = prevs.reshape(nblocks, BL)[:, 0]

    def onward_traversal(acceptance_line_tile, lookup_line_tile, payload_line_tile, source_line_tile, reward_array):

        def step(evolving_memory, item):
            acceptance_division, lookup_division, payload_division, source_division, memory_division, location_division = item
            concluding_answer, evolving_memory = tile_advance_update(acceptance_division, lookup_division, payload_division, source_division, reward_array, memory_division, location_division, evolving_memory)
            return (evolving_memory, concluding_answer)
        items = (acceptance_line_tile.reshape(nblocks, BL, FEATURE_DIM), lookup_line_tile.reshape(nblocks, BL, FEATURE_DIM), payload_line_tile.reshape(nblocks, BL, FEATURE_DIM), source_line_tile.reshape(nblocks, BL, FEATURE_DIM), seg_blocks, prev_blocks)
        start = jnp.zeros((HEADS, HS, HS), jnp.float32)
        spare_placeholder, results = lax.scan(jax.checkpoint(step), start, items)
        return results.reshape(TOKENS, FEATURE_DIM)
    spare_placeholder, adjoint_mapping = jax.vjp(onward_traversal, acceptance_gate.astype(jnp.float32), lookup_matrix.astype(jnp.float32), payload_matrix.astype(jnp.float32), fading_parameter, present_reward)
    derivative_bundle = adjoint_mapping(emitted_cotangent.astype(jnp.float32))
    return (derivative_bundle[0].astype(jnp.bfloat16), derivative_bundle[1].astype(jnp.bfloat16), derivative_bundle[2].astype(jnp.bfloat16), derivative_bundle[3].astype(jnp.bfloat16), derivative_bundle[4])
```

```python
import functools

import jax
import jax.numpy as jnp
from jax import lax
from jax.experimental import pallas as pl
from jax.experimental.pallas import tpu as pltpu
from jax.sharding import PartitionSpec as P

HS = 64
LANES = 128
HALF = 32
BLOCK_ROWS = 72
GROUPS = 4
MESH = pl.DeviceIdType.MESH
F32 = jnp.float32
BF16 = jnp.bfloat16


def split2(x):
    hi = x.astype(BF16)
    lo = (x - hi.astype(F32)).astype(BF16)
    return hi, lo


def split3(x):
    hi = x.astype(BF16)
    rest = x - hi.astype(F32)
    mid = rest.astype(BF16)
    lo = (rest - mid.astype(F32)).astype(BF16)
    return hi, mid, lo


def lanes(*xs):
    return jnp.concatenate(xs, axis=1)


def rows(*xs):
    return jnp.concatenate(xs, axis=0)


def dot(a, b):
    return lax.dot_general(a, b, (((1,), (0,)), ((), ())), preferred_element_type=F32)


def dot_nt(a, b):
    return lax.dot_general(a, b, (((1,), (1,)), ((), ())), preferred_element_type=F32)


def kernel(
    n,
    r_ref,
    k_ref,
    v_ref,
    x_ref,
    u_ref,
    dy_ref,
    spans_ref,
    dr_ref,
    dk_ref,
    dv_ref,
    dx_ref,
    du_ref,
    lw_s,
    cum_s,
    dyv_s,
    dq_s,
    dkk_s,
    dvv_s,
    mask_s,
    maskt_s,
    carried_s,
    keep_s,
    flag_s,
    blk,
    rx1,
    tx2,
    rx2,
    tot,
    rx3f,
    rx3b,
    rx3t,
    tx4,
    rx4,
    tx5,
    fin,
    core_send,
    core_recv,
    send2,
    recv2,
    send3,
    recv3,
    send3t,
    recv3t,
    send4,
    recv4,
):
    tokens, width = r_ref.shape
    pairs = width // LANES
    group_size = n // GROUPS
    chips = group_size // 2
    piece = width // chips
    me = lax.axis_index("seq")
    core = lax.rem(me, 2)
    chip = lax.rem(me // 2, chips)
    group = me // group_size
    partner = me + 1 - 2 * core

    def at_chip(offset):
        target = lax.rem(chip + offset, chips)
        return target, group * group_size + target * 2 + core

    def at_group(offset):
        return lax.rem(group + offset, GROUPS) * group_size + chip * 2 + core

    barrier = pltpu.get_barrier_semaphore()
    friends = [partner]
    friends += [at_chip(o)[1] for o in range(1, chips)]
    friends += [at_group(o) for o in range(1, GROUPS)]
    for friend in friends:
        pl.semaphore_signal(barrier, inc=1, device_id=(friend,), device_id_type=MESH)

    docs = spans_ref.shape[1]
    spans_row = spans_ref[...].astype(F32)
    one = lax.broadcasted_iota(jnp.int32, (docs, docs), 0)
    two = lax.broadcasted_iota(jnp.int32, (docs, docs), 1)
    spread = jnp.broadcast_to(spans_row, (docs, docs))
    spans_col = jnp.sum(jnp.where(one == two, spread, 0.0), axis=1, keepdims=True)
    starts_col = jnp.sum(jnp.where(two < one, spread, 0.0), axis=1, keepdims=True)
    starts_row = jnp.sum(jnp.where(one < two, spans_col, 0.0), axis=0, keepdims=True)
    base = (me * tokens).astype(F32)
    pos_col = base + lax.broadcasted_iota(jnp.int32, (tokens, 1), 0).astype(F32)
    pos_row = base + lax.broadcasted_iota(jnp.int32, (1, tokens), 1).astype(F32)
    seg_col = jnp.sum((starts_row <= pos_col).astype(F32), axis=1, keepdims=True)
    seg_row = jnp.sum((starts_col <= pos_row).astype(F32), axis=0, keepdims=True)
    seg_prev = jnp.sum((starts_row <= base - 1.0).astype(F32), axis=1, keepdims=True)
    seg_last = jnp.sum(
        (starts_row <= base + (tokens - 1.0)).astype(F32), axis=1, keepdims=True
    )
    first = lax.broadcasted_iota(jnp.int32, (tokens, tokens), 0)
    second = lax.broadcasted_iota(jnp.int32, (tokens, tokens), 1)
    same = seg_col == seg_row
    mask = jnp.where((first > second) & same, 1.0, 0.0)
    maskt = jnp.where((second > first) & same, 1.0, 0.0)
    mask_s[...] = rows(mask, mask)
    maskt_s[...] = rows(maskt, maskt)
    carried_s[...] = jnp.broadcast_to((seg_col == seg_prev).astype(F32), (tokens, LANES))
    keep_s[...] = jnp.broadcast_to((seg_col == seg_last).astype(F32), (tokens, LANES))
    flag_s[...] = jnp.broadcast_to((seg_last == seg_prev).astype(F32), (8, LANES))

    lane = lax.broadcasted_iota(jnp.int32, (1, LANES), 1)
    in_a = lane < HS
    mask_a = in_a.astype(F32).astype(BF16)
    mask_b = (1.0 - in_a.astype(F32)).astype(BF16)
    lower = jnp.where(first >= second, 1.0, 0.0).astype(BF16)
    upper = jnp.where(first <= second, 1.0, 0.0).astype(BF16)
    lower3 = lanes(lower, lower, lower)
    upper3 = lanes(upper, upper, upper)
    head_i = lax.broadcasted_iota(jnp.int32, (LANES, LANES), 0) // HS
    head_j = lax.broadcasted_iota(jnp.int32, (LANES, LANES), 1) // HS
    ones = jnp.where(head_i == head_j, 1.0, 0.0).astype(BF16)
    ones2 = rows(ones, ones)
    ones3 = rows(ones, ones, ones)

    def stacked(x):
        return rows(x * mask_a, x * mask_b)

    def pick(x):
        m = x.shape[0] // 2
        return jnp.where(in_a, x[:m], x[m:])

    def where_of(p):
        cols = pl.ds(pl.multiple_of(p * LANES, LANES), LANES)
        per = piece // LANES
        sub = pl.ds(pl.multiple_of(lax.rem(p, per) * LANES, LANES), LANES)
        return cols, p // per, sub

    def summarise(p):
        cols, slot, sub = where_of(p)
        r, k = r_ref[:, cols].astype(F32), k_ref[:, cols].astype(F32)
        v, dy = v_ref[:, cols], dy_ref[:, cols]
        lw = -jnp.exp(x_ref[:, cols])
        cum = dot(lower3, rows(*split3(lw)))
        lw_s[:, cols] = lw
        cum_s[:, cols] = cum
        last = cum[tokens - 1 : tokens]
        ending = k * jnp.exp(last - cum) * keep_s[...]
        reached = r * jnp.exp(cum - lw) * carried_s[...]
        vt, dyt = v.T, dy.T
        ends = pick(dot(lanes(vt, vt), rows(*split2(ending))))
        pulls = pick(dot(lanes(dyt, dyt), rows(*split2(reached))))
        dyv = dot(lanes(*split2(dy.astype(F32) * v.astype(F32))), ones2)
        dyv_s[:, cols] = dyv
        du = jnp.sum(dyv * r * k, axis=0, keepdims=True)
        through = jnp.exp(last) * flag_s[0:1]
        tail = rows(through, du, jnp.zeros((6, LANES), F32))
        for h in range(2):
            blk[h, slot, 0:HALF, sub] = ends[h * HALF : (h + 1) * HALF]
            blk[h, slot, HALF : 2 * HALF, sub] = pulls[h * HALF : (h + 1) * HALF]
            blk[h, slot, 2 * HALF : BLOCK_ROWS, sub] = tail

    def local_part(p):
        cols, _, _ = where_of(p)
        r, k = r_ref[:, cols].astype(F32), k_ref[:, cols].astype(F32)
        v, dy = v_ref[:, cols], dy_ref[:, cols]
        lw, cum = lw_s[:, cols], cum_s[:, cols]
        qh, ql = split2(r * jnp.exp(cum - lw))
        kh, kl = split2(k * jnp.exp(-cum))
        kh2, kl2 = stacked(kh), stacked(kl)
        at = dot_nt(lanes(kh2, kl2, kh2), lanes(qh, qh, ql))
        at = jnp.where(maskt_s[...] > 0.0, at, 0.0)
        da = jnp.where(mask_s[...] > 0.0, dot_nt(stacked(dy), v), 0.0)
        dat = jnp.where(maskt_s[...] > 0.0, dot_nt(stacked(v), dy), 0.0)
        dvv_s[:, cols] = pick(dot(lanes(*split2(at)), rows(dy, dy)))
        dah, dal = split2(da)
        dq_s[:, cols] = pick(dot(lanes(dah, dal, dah), rows(kh, kh, kl)))
        dth, dtl = split2(dat)
        dkk_s[:, cols] = pick(dot(lanes(dth, dtl, dth), rows(qh, qh, ql)))

    def finish(p):
        cols, slot, sub = where_of(p)
        r, k = r_ref[:, cols].astype(F32), k_ref[:, cols].astype(F32)
        v, dy = v_ref[:, cols], dy_ref[:, cols]
        u = u_ref[:, cols]
        lw, cum, dyv = lw_s[:, cols], cum_s[:, cols], dyv_s[:, cols]
        s = rows(fin[0, slot, 0:HALF, sub], fin[1, slot, 0:HALF, sub])
        g = rows(fin[0, slot, HALF : 2 * HALF, sub], fin[1, slot, HALF : 2 * HALF, sub])
        sh, sl = split2(rows(jnp.where(in_a, s, 0.0), jnp.where(in_a, 0.0, s)))
        gh, gl = split2(rows(jnp.where(in_a, g, 0.0), jnp.where(in_a, 0.0, g)))
        dq = dq_s[:, cols] + dot(lanes(dy, dy), rows(sh, sl)) * carried_s[...]
        de = dot(lanes(v, v), rows(gh, gl))
        last = cum[tokens - 1 : tokens]
        fade = jnp.exp(last - cum) * keep_s[...]
        ending = k * fade
        eh, el = split2(ending)
        eb, enc = jnp.exp(cum - lw), jnp.exp(-cum)
        bonus = dot(lanes(*split3(r * u * k)), ones3)
        dkk = dkk_s[:, cols]
        dv = dvv_s[:, cols] + dot_nt(lanes(eh, el, eh), lanes(gh, gh, gl))
        dv = dv + bonus * dy.astype(F32)
        du = dyv * u
        dr_ref[:, cols] = (dq * eb + du * k).astype(BF16)
        dk_ref[:, cols] = (dkk * enc + de * fade + du * r).astype(BF16)
        dv_ref[:, cols] = dv.astype(BF16)
        db = dq * (r * eb)
        ee = de * ending
        through = jnp.exp(last) * flag_s[0:1]
        tail = jnp.sum(ee, axis=0, keepdims=True)
        tail = tail + through * jnp.sum(s * g, axis=0, keepdims=True)
        total = db - dkk * (k * enc) - ee
        rev = dot(upper3, rows(*split3(total))) + tail - db
        dx_ref[:, cols] = (rev * lw).astype(BF16)
        du_ref[:, cols] = fin[0, slot, 2 * HALF + 1 : 2 * HALF + 2, sub]

    def run(part, low, high):
        def step(i, carry):
            part(2 * i)
            part(2 * i + 1)
            return carry

        lax.fori_loop(low, high, step, 0)

    cuts = [pairs * c // 16 for c in (0, 1, 4, 5, 7, 8)]
    run(summarise, 0, pairs // 2)

    def remote(src, dst, send, recv, device):
        return pltpu.make_async_remote_copy(
            src_ref=src,
            dst_ref=dst,
            send_sem=send,
            recv_sem=recv,
            device_id=(device,),
            device_id_type=MESH,
        )

    pl.semaphore_wait(barrier, len(friends))

    copy1 = remote(blk.at[1 - core], rx1, core_send.at[0], core_recv.at[0], partner)
    copy1.start()
    run(local_part, cuts[0], cuts[1])
    copy1.wait_recv()
    late = core == 1
    e_rows, p_rows = slice(0, HALF), slice(HALF, 2 * HALF)
    t_row, u_row = slice(2 * HALF, 2 * HALF + 1), slice(2 * HALF + 1, 2 * HALF + 2)
    end_rows = slice(2 * HALF, BLOCK_ROWS)

    def tail_of(t, u):
        return rows(t, u, jnp.zeros((6, piece), F32))

    def combine(c, carry):
        ta, tb = blk[core, c, t_row], rx1[c, t_row]
        ea, eb = blk[core, c, e_rows], rx1[c, e_rows]
        pa, pb = blk[core, c, p_rows], rx1[c, p_rows]
        tx2[c, e_rows] = jnp.where(late, ta * eb + ea, tb * ea + eb)
        tx2[c, p_rows] = jnp.where(late, pb + tb * pa, pa + ta * pb)
        tx2[c, end_rows] = tail_of(ta * tb, blk[core, c, u_row] + rx1[c, u_row])
        return carry

    lax.fori_loop(0, chips, combine, 0)

    copies2 = []
    for o in range(1, chips):
        target, device = at_chip(o)
        copies2.append(
            remote(tx2.at[target], rx2.at[chip], send2.at[o], recv2.at[o], device)
        )
        copies2[-1].start()
    rx2[chip] = tx2[chip]
    run(local_part, cuts[1], cuts[2])
    for copy in copies2:
        copy.wait_recv()

    def forward(c, carry):
        f, t, du = carry
        tx4[c, e_rows] = f
        tc = rx2[c, t_row]
        tx4[c, t_row] = t
        return tc * f + rx2[c, e_rows], t * tc, du + rx2[c, u_row]

    zero, row = jnp.zeros((HALF, piece), F32), jnp.zeros((1, piece), F32)
    f, t, du = lax.fori_loop(0, chips, forward, (zero, row + 1.0, row))

    def backward(i, carry):
        c = chips - 1 - i
        b, t = carry
        tx4[c, p_rows] = b
        tc = rx2[c, t_row]
        tx4[c, u_row] = t
        return rx2[c, p_rows] + tc * b, t * tc

    b, t = lax.fori_loop(0, chips, backward, (zero, row + 1.0))
    tot[e_rows] = f
    tot[p_rows] = b
    tot[end_rows] = tail_of(t, du)

    ahead = remote(tot.at[e_rows], rx3f, send3.at[0], recv3.at[0], at_group(1))
    behind = remote(
        tot.at[p_rows], rx3b, send3.at[1], recv3.at[1], at_group(GROUPS - 1)
    )
    has_next, has_prev = group < GROUPS - 1, group > 0

    @pl.when(has_next)
    def _():
        ahead.start()

    @pl.when(has_prev)
    def _():
        behind.start()

    copies3 = []
    for o in range(1, GROUPS):
        copies3.append(
            remote(
                tot.at[end_rows],
                rx3t.at[o - 1],
                send3t.at[o - 1],
                recv3t.at[o - 1],
                at_group(o),
            )
        )
        copies3[-1].start()
    run(local_part, cuts[2], cuts[3])

    @pl.when(has_prev)
    def _():
        ahead.wait_recv()

    @pl.when(jnp.logical_not(has_prev))
    def _():
        rx3f[...] = zero

    @pl.when(has_next)
    def _():
        behind.wait_recv()

    @pl.when(jnp.logical_not(has_next))
    def _():
        rx3b[...] = zero

    for copy in copies3:
        copy.wait_recv()
    du = tot[u_row]
    for o in range(1, GROUPS):
        du = du + rx3t[o - 1, 1:2]

    def carry_in(c, carry):
        tx4[c, e_rows] = tx4[c, e_rows] + tx4[c, t_row] * rx3f[...]
        tx4[c, p_rows] = tx4[c, p_rows] + tx4[c, u_row] * rx3b[...]
        tx4[c, end_rows] = tail_of(row, du)
        return carry

    lax.fori_loop(0, chips, carry_in, 0)

    copies4 = []
    for o in range(1, chips):
        target, device = at_chip(o)
        copies4.append(
            remote(tx4.at[target], rx4.at[chip], send4.at[o], recv4.at[o], device)
        )
        copies4[-1].start()
    rx4[chip] = tx4[chip]
    run(local_part, cuts[3], cuts[4])
    for copy in copies4:
        copy.wait_recv()

    def share(c, carry):
        ta, tb = blk[core, c, t_row], rx1[c, t_row]
        ea, eb = blk[core, c, e_rows], rx1[c, e_rows]
        pa, pb = blk[core, c, p_rows], rx1[c, p_rows]
        fc, bc, end = rx4[c, e_rows], rx4[c, p_rows], rx4[c, end_rows]
        fin[core, c, e_rows] = jnp.where(late, tb * fc + eb, fc)
        fin[core, c, p_rows] = jnp.where(late, bc, pb + tb * bc)
        fin[core, c, end_rows] = end
        tx5[c, e_rows] = jnp.where(late, fc, ta * fc + ea)
        tx5[c, p_rows] = jnp.where(late, pa + ta * bc, bc)
        tx5[c, end_rows] = end
        return carry

    lax.fori_loop(0, chips, share, 0)
    copy5 = remote(tx5, fin.at[core], core_send.at[1], core_recv.at[1], partner)
    copy5.start()
    run(local_part, cuts[4], cuts[5])
    copy5.wait_recv()
    run(finish, 0, pairs // 2)

    copy1.wait_send()
    for copy in copies2 + copies3 + copies4:
        copy.wait_send()
    copy5.wait_send()

    @pl.when(has_next)
    def _():
        ahead.wait_send()

    @pl.when(has_prev)
    def _():
        behind.wait_send()


def body(
    n,
    acceptance_gate,
    lookup_matrix,
    payload_matrix,
    fading_parameter,
    present_reward,
    emitted_cotangent,
    paper_spans,
):
    tokens, width = acceptance_gate.shape
    chips = n // GROUPS // 2
    piece = width // chips
    full = pltpu.VMEM((tokens, width), F32)
    table = pltpu.VMEM((tokens, LANES), F32)
    table2 = pltpu.VMEM((2 * tokens, LANES), F32)
    half = pltpu.VMEM((chips, BLOCK_ROWS, piece), F32)
    both = pltpu.VMEM((2, chips, BLOCK_ROWS, piece), F32)
    state = pltpu.VMEM((HALF, piece), F32)
    sems = pltpu.SemaphoreType.DMA
    grad = jax.ShapeDtypeStruct((tokens, width), BF16)
    outs = pl.pallas_call(
        functools.partial(kernel, n),
        out_shape=(grad, grad, grad, grad, jax.ShapeDtypeStruct((1, width), F32)),
        in_specs=[pl.BlockSpec(memory_space=pltpu.VMEM)] * 7,
        out_specs=[pl.BlockSpec(memory_space=pltpu.VMEM)] * 5,
        scratch_shapes=[full] * 6
        + [table2, table2, table, table, pltpu.VMEM((8, LANES), F32)]
        + [both, half, half, half, pltpu.VMEM((BLOCK_ROWS, piece), F32)]
        + [state, state, pltpu.VMEM((GROUPS - 1, 8, piece), F32)]
        + [half, half, half, both]
        + [sems((2,)), sems((2,)), sems((chips,)), sems((chips,))]
        + [sems((2,)), sems((2,)), sems((GROUPS - 1,)), sems((GROUPS - 1,))]
        + [sems((chips,)), sems((chips,))],
        compiler_params=pltpu.CompilerParams(
            collective_id=0,
            has_side_effects=True,
            vmem_limit_bytes=44 * 1024 * 1024,
        ),
    )(
        acceptance_gate,
        lookup_matrix,
        payload_matrix,
        fading_parameter,
        present_reward.reshape(1, width),
        emitted_cotangent,
        paper_spans.reshape(1, -1),
    )
    return (*outs[:4], outs[4].reshape(width))


def solution(mesh):
    row = P("seq", None)
    return jax.shard_map(
        functools.partial(body, mesh.shape["seq"]),
        mesh=mesh,
        in_specs=(row, row, row, row, P(), row, P()),
        out_specs=(row, row, row, row, P()),
        check_vma=False,
    )
```

```python
import functools

import jax
import jax.numpy as jnp
from jax import lax
from jax.experimental import pallas as pl
from jax.experimental.pallas import tpu as pltpu
from jax.sharding import PartitionSpec as P

HS = 64
LANES = 128
HALF = 32
BLOCK_ROWS = 72
GROUPS = 4
MESH = pl.DeviceIdType.MESH
F32 = jnp.float32
BF16 = jnp.bfloat16


def split2(x):
    hi = x.astype(BF16)
    lo = (x - hi.astype(F32)).astype(BF16)
    return hi, lo


def split3(x):
    hi = x.astype(BF16)
    rest = x - hi.astype(F32)
    mid = rest.astype(BF16)
    lo = (rest - mid.astype(F32)).astype(BF16)
    return hi, mid, lo


def lanes(*xs):
    return jnp.concatenate(xs, axis=1)


def rows(*xs):
    return jnp.concatenate(xs, axis=0)


def dot(a, b):
    return lax.dot_general(a, b, (((1,), (0,)), ((), ())), preferred_element_type=F32)


def dot_nt(a, b):
    return lax.dot_general(a, b, (((1,), (1,)), ((), ())), preferred_element_type=F32)


def kernel(
    n,
    r_hbm,
    k_hbm,
    v_hbm,
    x_hbm,
    u_hbm,
    dy_hbm,
    spans_hbm,
    dr_ref,
    dk_ref,
    dv_ref,
    dx_ref,
    du_ref,
    r_ref,
    k_ref,
    v_ref,
    x_ref,
    u_ref,
    dy_ref,
    spans_ref,
    lw_s,
    cum_s,
    dyv_s,
    dq_s,
    dkk_s,
    dvv_s,
    mask_s,
    maskt_s,
    carried_s,
    keep_s,
    flag_s,
    blk,
    rx1,
    tx2,
    rx2,
    tot,
    rx3f,
    rx3b,
    rx3t,
    tx4,
    rx4,
    tx5,
    fin,
    in_sem,
    small_sem,
    core_send,
    core_recv,
    send2,
    recv2,
    send3,
    recv3,
    send3t,
    recv3t,
    send4,
    recv4,
):
    tokens, width = r_ref.shape
    pairs = width // LANES
    group_size = n // GROUPS
    chips = group_size // 2
    piece = width // chips
    me = lax.axis_index("seq")
    core = lax.rem(me, 2)
    chip = lax.rem(me // 2, chips)
    group = me // group_size
    partner = me + 1 - 2 * core

    def at_chip(offset):
        target = lax.rem(chip + offset, chips)
        return target, group * group_size + target * 2 + core

    def at_group(offset):
        return lax.rem(group + offset, GROUPS) * group_size + chip * 2 + core

    barrier = pltpu.get_barrier_semaphore()
    friends = [partner]
    friends += [at_chip(o)[1] for o in range(1, chips)]
    friends += [at_group(o) for o in range(1, GROUPS)]
    for friend in friends:
        pl.semaphore_signal(barrier, inc=1, device_id=(friend,), device_id_type=MESH)

    load_spans = pltpu.make_async_copy(spans_hbm, spans_ref, small_sem.at[0])
    load_u = pltpu.make_async_copy(u_hbm, u_ref, small_sem.at[1])
    load_spans.start()
    load_u.start()
    large = (
        (x_hbm, x_ref),
        (k_hbm, k_ref),
        (r_hbm, r_ref),
        (v_hbm, v_ref),
        (dy_hbm, dy_ref),
    )
    loads = []
    for o in range(1, chips + 1):
        target = lax.rem(chip + o, chips)
        cols = pl.ds(pl.multiple_of(target * piece, LANES), piece)
        loads.append(
            [
                pltpu.make_async_copy(
                    src.at[:, cols], dst.at[:, cols], in_sem.at[i * chips + o - 1]
                )
                for i, (src, dst) in enumerate(large)
            ]
        )
        for load in loads[-1]:
            load.start()

    load_spans.wait()
    docs = spans_ref.shape[1]
    spans_row = spans_ref[...].astype(F32)
    one = lax.broadcasted_iota(jnp.int32, (docs, docs), 0)
    two = lax.broadcasted_iota(jnp.int32, (docs, docs), 1)
    spread = jnp.broadcast_to(spans_row, (docs, docs))
    spans_col = jnp.sum(jnp.where(one == two, spread, 0.0), axis=1, keepdims=True)
    starts_col = jnp.sum(jnp.where(two < one, spread, 0.0), axis=1, keepdims=True)
    starts_row = jnp.sum(jnp.where(one < two, spans_col, 0.0), axis=0, keepdims=True)
    base = (me * tokens).astype(F32)
    pos_col = base + lax.broadcasted_iota(jnp.int32, (tokens, 1), 0).astype(F32)
    pos_row = base + lax.broadcasted_iota(jnp.int32, (1, tokens), 1).astype(F32)
    seg_col = jnp.sum((starts_row <= pos_col).astype(F32), axis=1, keepdims=True)
    seg_row = jnp.sum((starts_col <= pos_row).astype(F32), axis=0, keepdims=True)
    seg_prev = jnp.sum((starts_row <= base - 1.0).astype(F32), axis=1, keepdims=True)
    seg_last = jnp.sum(
        (starts_row <= base + (tokens - 1.0)).astype(F32), axis=1, keepdims=True
    )
    first = lax.broadcasted_iota(jnp.int32, (tokens, tokens), 0)
    second = lax.broadcasted_iota(jnp.int32, (tokens, tokens), 1)
    same = seg_col == seg_row
    mask = jnp.where((first > second) & same, 1.0, 0.0)
    maskt = jnp.where((second > first) & same, 1.0, 0.0)
    mask_s[...] = rows(mask, mask)
    maskt_s[...] = rows(maskt, maskt)
    carried_s[...] = jnp.broadcast_to((seg_col == seg_prev).astype(F32), (tokens, LANES))
    keep_s[...] = jnp.broadcast_to((seg_col == seg_last).astype(F32), (tokens, LANES))
    flag_s[...] = jnp.broadcast_to((seg_last == seg_prev).astype(F32), (8, LANES))

    lane = lax.broadcasted_iota(jnp.int32, (1, LANES), 1)
    in_a = lane < HS
    mask_a = in_a.astype(F32).astype(BF16)
    mask_b = (1.0 - in_a.astype(F32)).astype(BF16)
    lower = jnp.where(first >= second, 1.0, 0.0).astype(BF16)
    upper = jnp.where(first <= second, 1.0, 0.0).astype(BF16)
    lower3 = lanes(lower, lower, lower)
    upper3 = lanes(upper, upper, upper)
    head_i = lax.broadcasted_iota(jnp.int32, (LANES, LANES), 0) // HS
    head_j = lax.broadcasted_iota(jnp.int32, (LANES, LANES), 1) // HS
    ones = jnp.where(head_i == head_j, 1.0, 0.0).astype(BF16)
    ones2 = rows(ones, ones)
    ones3 = rows(ones, ones, ones)

    def stacked(x):
        return rows(x * mask_a, x * mask_b)

    def pick(x):
        m = x.shape[0] // 2
        return jnp.where(in_a, x[:m], x[m:])

    def where_of(p):
        cols = pl.ds(pl.multiple_of(p * LANES, LANES), LANES)
        per = piece // LANES
        sub = pl.ds(pl.multiple_of(lax.rem(p, per) * LANES, LANES), LANES)
        return cols, p // per, sub

    def summarise(p):
        cols, slot, sub = where_of(p)
        r, k = r_ref[:, cols].astype(F32), k_ref[:, cols].astype(F32)
        v, dy = v_ref[:, cols], dy_ref[:, cols]
        lw = -jnp.exp(x_ref[:, cols])
        cum = dot(lower3, rows(*split3(lw)))
        lw_s[:, cols] = lw
        cum_s[:, cols] = cum
        last = cum[tokens - 1 : tokens]
        ending = k * jnp.exp(last - cum) * keep_s[...]
        reached = r * jnp.exp(cum - lw) * carried_s[...]
        vt, dyt = v.T, dy.T
        ends = pick(dot(lanes(vt, vt), rows(*split2(ending))))
        pulls = pick(dot(lanes(dyt, dyt), rows(*split2(reached))))
        dyv = dot(lanes(*split2(dy.astype(F32) * v.astype(F32))), ones2)
        dyv_s[:, cols] = dyv
        du = jnp.sum(dyv * r * k, axis=0, keepdims=True)
        through = jnp.exp(last) * flag_s[0:1]
        tail = rows(through, du, jnp.zeros((6, LANES), F32))
        for h in range(2):
            blk[h, slot, 0:HALF, sub] = ends[h * HALF : (h + 1) * HALF]
            blk[h, slot, HALF : 2 * HALF, sub] = pulls[h * HALF : (h + 1) * HALF]
            blk[h, slot, 2 * HALF : BLOCK_ROWS, sub] = tail

    def local_part(p):
        cols, _, _ = where_of(p)
        r, k = r_ref[:, cols].astype(F32), k_ref[:, cols].astype(F32)
        v, dy = v_ref[:, cols], dy_ref[:, cols]
        lw, cum = lw_s[:, cols], cum_s[:, cols]
        qh, ql = split2(r * jnp.exp(cum - lw))
        kh, kl = split2(k * jnp.exp(-cum))
        kh2, kl2 = stacked(kh), stacked(kl)
        at = dot_nt(lanes(kh2, kl2, kh2), lanes(qh, qh, ql))
        at = jnp.where(maskt_s[...] > 0.0, at, 0.0)
        da = jnp.where(mask_s[...] > 0.0, dot_nt(stacked(dy), v), 0.0)
        dat = jnp.where(maskt_s[...] > 0.0, dot_nt(stacked(v), dy), 0.0)
        dvv_s[:, cols] = pick(dot(lanes(*split2(at)), rows(dy, dy)))
        dah, dal = split2(da)
        dq_s[:, cols] = pick(dot(lanes(dah, dal, dah), rows(kh, kh, kl)))
        dth, dtl = split2(dat)
        dkk_s[:, cols] = pick(dot(lanes(dth, dtl, dth), rows(qh, qh, ql)))

    def finish(p):
        cols, slot, sub = where_of(p)
        r, k = r_ref[:, cols].astype(F32), k_ref[:, cols].astype(F32)
        v, dy = v_ref[:, cols], dy_ref[:, cols]
        u = u_ref[:, cols]
        lw, cum, dyv = lw_s[:, cols], cum_s[:, cols], dyv_s[:, cols]
        s = rows(fin[0, slot, 0:HALF, sub], fin[1, slot, 0:HALF, sub])
        g = rows(fin[0, slot, HALF : 2 * HALF, sub], fin[1, slot, HALF : 2 * HALF, sub])
        sh, sl = split2(rows(jnp.where(in_a, s, 0.0), jnp.where(in_a, 0.0, s)))
        gh, gl = split2(rows(jnp.where(in_a, g, 0.0), jnp.where(in_a, 0.0, g)))
        dq = dq_s[:, cols] + dot(lanes(dy, dy), rows(sh, sl)) * carried_s[...]
        de = dot(lanes(v, v), rows(gh, gl))
        last = cum[tokens - 1 : tokens]
        fade = jnp.exp(last - cum) * keep_s[...]
        ending = k * fade
        eh, el = split2(ending)
        eb, enc = jnp.exp(cum - lw), jnp.exp(-cum)
        bonus = dot(lanes(*split3(r * u * k)), ones3)
        dkk = dkk_s[:, cols]
        dv = dvv_s[:, cols] + dot_nt(lanes(eh, el, eh), lanes(gh, gh, gl))
        dv = dv + bonus * dy.astype(F32)
        du = dyv * u
        dr_ref[:, cols] = (dq * eb + du * k).astype(BF16)
        dk_ref[:, cols] = (dkk * enc + de * fade + du * r).astype(BF16)
        dv_ref[:, cols] = dv.astype(BF16)
        db = dq * (r * eb)
        ee = de * ending
        through = jnp.exp(last) * flag_s[0:1]
        tail = jnp.sum(ee, axis=0, keepdims=True)
        tail = tail + through * jnp.sum(s * g, axis=0, keepdims=True)
        total = db - dkk * (k * enc) - ee
        rev = dot(upper3, rows(*split3(total))) + tail - db
        dx_ref[:, cols] = (rev * lw).astype(BF16)
        du_ref[:, cols] = fin[0, slot, 2 * HALF + 1 : 2 * HALF + 2, sub]

    per = piece // LANES

    def run(part, low, count):
        if count % 2:
            for i in range(count):
                part(low + i)
            return

        def step(i, carry):
            part(low + 2 * i)
            part(low + 2 * i + 1)
            return carry

        lax.fori_loop(0, count // 2, step, 0)

    cuts = [pairs * c // 16 for c in (0, 2, 6, 10, 14, 16)]

    def remote(src, dst, send, recv, device):
        return pltpu.make_async_remote_copy(
            src_ref=src,
            dst_ref=dst,
            send_sem=send,
            recv_sem=recv,
            device_id=(device,),
            device_id_type=MESH,
        )

    late = core == 1
    e_rows, p_rows = slice(0, HALF), slice(HALF, 2 * HALF)
    t_row, u_row = slice(2 * HALF, 2 * HALF + 1), slice(2 * HALF + 1, 2 * HALF + 2)
    end_rows = slice(2 * HALF, BLOCK_ROWS)

    def tail_of(t, u):
        return rows(t, u, jnp.zeros((6, piece), F32))

    def combine(c, out):
        ta, tb = blk[core, c, t_row], rx1[c, t_row]
        ea, eb = blk[core, c, e_rows], rx1[c, e_rows]
        pa, pb = blk[core, c, p_rows], rx1[c, p_rows]
        out[c, e_rows] = jnp.where(late, ta * eb + ea, tb * ea + eb)
        out[c, p_rows] = jnp.where(late, pb + tb * pa, pa + ta * pb)
        out[c, end_rows] = tail_of(ta * tb, blk[core, c, u_row] + rx1[c, u_row])

    copies1, copies2 = [], []

    def pass_on(o):
        copies1[o - 1].wait_recv()
        target, device = at_chip(o)
        if o == chips:
            combine(chip, rx2)
            return
        combine(target, tx2)
        copies2.append(
            remote(tx2.at[target], rx2.at[chip], send2.at[o], recv2.at[o], device)
        )
        copies2[-1].start()

    for o in range(1, chips + 1):
        target, _ = at_chip(o)
        for load in loads[o - 1]:
            load.wait()
        run(summarise, target * per, per)
        if o == 1:
            pl.semaphore_wait(barrier, len(friends))
        copies1.append(
            remote(
                blk.at[1 - core, target],
                rx1.at[target],
                core_send.at[o - 1],
                core_recv.at[o - 1],
                partner,
            )
        )
        copies1[-1].start()
        if o > 1:
            pass_on(o - 1)
    run(local_part, cuts[0], cuts[1] - cuts[0])
    pass_on(chips)
    run(local_part, cuts[1], cuts[2] - cuts[1])
    for copy in copies2:
        copy.wait_recv()

    def forward(c, carry):
        f, t, du = carry
        tx4[c, e_rows] = f
        tc = rx2[c, t_row]
        tx4[c, t_row] = t
        return tc * f + rx2[c, e_rows], t * tc, du + rx2[c, u_row]

    zero, row = jnp.zeros((HALF, piece), F32), jnp.zeros((1, piece), F32)
    f, t, du = lax.fori_loop(0, chips, forward, (zero, row + 1.0, row))

    def backward(i, carry):
        c = chips - 1 - i
        b, t = carry
        tx4[c, p_rows] = b
        tc = rx2[c, t_row]
        tx4[c, u_row] = t
        return rx2[c, p_rows] + tc * b, t * tc

    b, t = lax.fori_loop(0, chips, backward, (zero, row + 1.0))
    tot[e_rows] = f
    tot[p_rows] = b
    tot[end_rows] = tail_of(t, du)

    ahead = remote(tot.at[e_rows], rx3f, send3.at[0], recv3.at[0], at_group(1))
    behind = remote(
        tot.at[p_rows], rx3b, send3.at[1], recv3.at[1], at_group(GROUPS - 1)
    )
    has_next, has_prev = group < GROUPS - 1, group > 0

    @pl.when(has_next)
    def _():
        ahead.start()

    @pl.when(has_prev)
    def _():
        behind.start()

    copies3 = []
    for o in range(1, GROUPS):
        copies3.append(
            remote(
                tot.at[end_rows],
                rx3t.at[o - 1],
                send3t.at[o - 1],
                recv3t.at[o - 1],
                at_group(o),
            )
        )
        copies3[-1].start()
    run(local_part, cuts[2], cuts[3] - cuts[2])

    @pl.when(has_prev)
    def _():
        ahead.wait_recv()

    @pl.when(jnp.logical_not(has_prev))
    def _():
        rx3f[...] = zero

    @pl.when(has_next)
    def _():
        behind.wait_recv()

    @pl.when(jnp.logical_not(has_next))
    def _():
        rx3b[...] = zero

    for copy in copies3:
        copy.wait_recv()
    du = tot[u_row]
    for o in range(1, GROUPS):
        du = du + rx3t[o - 1, 1:2]

    def carry_in(c, carry):
        tx4[c, e_rows] = tx4[c, e_rows] + tx4[c, t_row] * rx3f[...]
        tx4[c, p_rows] = tx4[c, p_rows] + tx4[c, u_row] * rx3b[...]
        tx4[c, end_rows] = tail_of(row, du)
        return carry

    lax.fori_loop(0, chips, carry_in, 0)

    copies4 = []
    for o in range(1, chips):
        target, device = at_chip(o)
        copies4.append(
            remote(tx4.at[target], rx4.at[chip], send4.at[o], recv4.at[o], device)
        )
        copies4[-1].start()
    rx4[chip] = tx4[chip]

    copies5 = []

    def share(o):
        c = lax.rem(chip - o + chips, chips)
        if o:
            copies4[o - 1].wait_recv()
        ta, tb = blk[core, c, t_row], rx1[c, t_row]
        ea, eb = blk[core, c, e_rows], rx1[c, e_rows]
        pa, pb = blk[core, c, p_rows], rx1[c, p_rows]
        fc, bc, end = rx4[c, e_rows], rx4[c, p_rows], rx4[c, end_rows]
        tx5[c, e_rows] = jnp.where(late, fc, ta * fc + ea)
        tx5[c, p_rows] = jnp.where(late, pa + ta * bc, bc)
        tx5[c, end_rows] = end
        copies5.append(
            remote(
                tx5.at[c],
                fin.at[core, c],
                core_send.at[chips + o],
                core_recv.at[chips + o],
                partner,
            )
        )
        copies5[-1].start()
        fin[core, c, e_rows] = jnp.where(late, tb * fc + eb, fc)
        fin[core, c, p_rows] = jnp.where(late, bc, pb + tb * bc)
        fin[core, c, end_rows] = end

    share(0)
    run(local_part, cuts[3], cuts[4] - cuts[3])
    share(1)
    run(local_part, cuts[4], cuts[5] - cuts[4])
    load_u.wait()
    for o in range(chips):
        if o + 2 < chips:
            share(o + 2)
        copies5[o].wait_recv()
        run(finish, lax.rem(chip - o + chips, chips) * per, per)

    for copy in copies1 + copies2 + copies3 + copies4 + copies5:
        copy.wait_send()

    @pl.when(has_next)
    def _():
        ahead.wait_send()

    @pl.when(has_prev)
    def _():
        behind.wait_send()


def body(
    n,
    acceptance_gate,
    lookup_matrix,
    payload_matrix,
    fading_parameter,
    present_reward,
    emitted_cotangent,
    paper_spans,
):
    tokens, width = acceptance_gate.shape
    chips = n // GROUPS // 2
    piece = width // chips
    full = pltpu.VMEM((tokens, width), F32)
    given = pltpu.VMEM((tokens, width), BF16)
    table = pltpu.VMEM((tokens, LANES), F32)
    table2 = pltpu.VMEM((2 * tokens, LANES), F32)
    half = pltpu.VMEM((chips, BLOCK_ROWS, piece), F32)
    both = pltpu.VMEM((2, chips, BLOCK_ROWS, piece), F32)
    state = pltpu.VMEM((HALF, piece), F32)
    sems = pltpu.SemaphoreType.DMA
    grad = jax.ShapeDtypeStruct((tokens, width), BF16)
    outs = pl.pallas_call(
        functools.partial(kernel, n),
        out_shape=(grad, grad, grad, grad, jax.ShapeDtypeStruct((1, width), F32)),
        in_specs=[pl.BlockSpec(memory_space=pltpu.HBM)] * 7,
        out_specs=[pl.BlockSpec(memory_space=pltpu.VMEM)] * 5,
        scratch_shapes=[given, given, given, full]
        + [pltpu.VMEM((1, width), F32), given]
        + [pltpu.VMEM((1, paper_spans.shape[0]), jnp.int32)]
        + [full] * 6
        + [table2, table2, table, table, pltpu.VMEM((8, LANES), F32)]
        + [both, half, half, half, pltpu.VMEM((BLOCK_ROWS, piece), F32)]
        + [state, state, pltpu.VMEM((GROUPS - 1, 8, piece), F32)]
        + [half, half, half, both]
        + [sems((5 * chips,)), sems((2,)), sems((2 * chips,)), sems((2 * chips,))]
        + [sems((chips,)), sems((chips,))]
        + [sems((2,)), sems((2,)), sems((GROUPS - 1,)), sems((GROUPS - 1,))]
        + [sems((chips,)), sems((chips,))],
        compiler_params=pltpu.CompilerParams(
            collective_id=0,
            has_side_effects=True,
            vmem_limit_bytes=44 * 1024 * 1024,
        ),
    )(
        acceptance_gate,
        lookup_matrix,
        payload_matrix,
        fading_parameter,
        present_reward.reshape(1, width),
        emitted_cotangent,
        paper_spans.reshape(1, -1),
    )
    return (*outs[:4], outs[4].reshape(width))


def solution(mesh):
    row = P("seq", None)
    return jax.shard_map(
        functools.partial(body, mesh.shape["seq"]),
        mesh=mesh,
        in_specs=(row, row, row, row, P(), row, P()),
        out_specs=(row, row, row, row, P()),
        check_vma=False,
    )
```

```python
import functools

import jax
import jax.numpy as jnp
from jax import lax
from jax.experimental import pallas as pl
from jax.experimental.pallas import tpu as pltpu
from jax.sharding import PartitionSpec as P

HS = 64
LANES = 128
HALF = 32
BLOCK_ROWS = 72
GROUPS = 4
VMEM_LIMIT = 62 * 1024 * 1024
MESH = pl.DeviceIdType.MESH
F32 = jnp.float32
BF16 = jnp.bfloat16


def split2(x):
    hi = x.astype(BF16)
    lo = (x - hi.astype(F32)).astype(BF16)
    return hi, lo


def split3(x):
    hi = x.astype(BF16)
    rest = x - hi.astype(F32)
    mid = rest.astype(BF16)
    lo = (rest - mid.astype(F32)).astype(BF16)
    return hi, mid, lo


def lanes(*xs):
    return jnp.concatenate(xs, axis=1)


def rows(*xs):
    return jnp.concatenate(xs, axis=0)


def dot(a, b):
    return lax.dot_general(a, b, (((1,), (0,)), ((), ())), preferred_element_type=F32)


def dot_nt(a, b):
    return lax.dot_general(a, b, (((1,), (1,)), ((), ())), preferred_element_type=F32)


def kernel(
    n,
    r_hbm,
    k_hbm,
    v_hbm,
    x_hbm,
    u_hbm,
    dy_hbm,
    spans_hbm,
    dr_hbm,
    dk_hbm,
    dv_hbm,
    dx_hbm,
    du_hbm,
    dr_ref,
    dk_ref,
    dv_ref,
    dx_ref,
    du_ref,
    r_ref,
    k_ref,
    v_ref,
    x_ref,
    u_ref,
    dy_ref,
    spans_ref,
    lw_s,
    cum_s,
    dyv_s,
    dq_s,
    dkk_s,
    dvv_s,
    mask_s,
    maskt_s,
    carried_s,
    keep_s,
    flag_s,
    blk,
    rx1,
    tx2,
    rx2,
    tot,
    rx3f,
    rx3b,
    rx3t,
    tx4,
    rx4,
    tx5,
    fin,
    in_sem,
    out_sem,
    small_sem,
    core_send,
    core_recv,
    send2,
    recv2,
    send3,
    recv3,
    send3t,
    recv3t,
    send4,
    recv4,
):
    tokens, width = r_ref.shape
    pairs = width // LANES
    group_size = n // GROUPS
    chips = group_size // 2
    piece = width // chips
    me = lax.axis_index("seq")
    core = lax.rem(me, 2)
    chip = lax.rem(me // 2, chips)
    group = me // group_size
    partner = me + 1 - 2 * core

    def at_chip(offset):
        target = lax.rem(chip + offset, chips)
        return target, group * group_size + target * 2 + core

    def at_group(offset):
        return lax.rem(group + offset, GROUPS) * group_size + chip * 2 + core

    barrier = pltpu.get_barrier_semaphore()
    friends = [partner]
    friends += [at_chip(o)[1] for o in range(1, chips)]
    friends += [at_group(o) for o in range(1, GROUPS)]
    for friend in friends:
        pl.semaphore_signal(barrier, inc=1, device_id=(friend,), device_id_type=MESH)

    load_spans = pltpu.make_async_copy(spans_hbm, spans_ref, small_sem.at[0])
    load_u = pltpu.make_async_copy(u_hbm, u_ref, small_sem.at[1])
    load_spans.start()
    load_u.start()
    large = (
        (x_hbm, x_ref),
        (k_hbm, k_ref),
        (r_hbm, r_ref),
        (v_hbm, v_ref),
        (dy_hbm, dy_ref),
    )
    loads = []
    for o in range(1, chips + 1):
        target = lax.rem(chip + o, chips)
        cols = pl.ds(pl.multiple_of(target * piece, LANES), piece)
        loads.append(
            [
                pltpu.make_async_copy(
                    src.at[:, cols], dst.at[:, cols], in_sem.at[i * chips + o - 1]
                )
                for i, (src, dst) in enumerate(large)
            ]
        )
        for load in loads[-1]:
            load.start()

    load_spans.wait()
    docs = spans_ref.shape[1]
    spans_row = spans_ref[...].astype(F32)
    one = lax.broadcasted_iota(jnp.int32, (docs, docs), 0)
    two = lax.broadcasted_iota(jnp.int32, (docs, docs), 1)
    spread = jnp.broadcast_to(spans_row, (docs, docs))
    spans_col = jnp.sum(jnp.where(one == two, spread, 0.0), axis=1, keepdims=True)
    starts_col = jnp.sum(jnp.where(two < one, spread, 0.0), axis=1, keepdims=True)
    starts_row = jnp.sum(jnp.where(one < two, spans_col, 0.0), axis=0, keepdims=True)
    base = (me * tokens).astype(F32)
    pos_col = base + lax.broadcasted_iota(jnp.int32, (tokens, 1), 0).astype(F32)
    pos_row = base + lax.broadcasted_iota(jnp.int32, (1, tokens), 1).astype(F32)
    seg_col = jnp.sum((starts_row <= pos_col).astype(F32), axis=1, keepdims=True)
    seg_row = jnp.sum((starts_col <= pos_row).astype(F32), axis=0, keepdims=True)
    seg_prev = jnp.sum((starts_row <= base - 1.0).astype(F32), axis=1, keepdims=True)
    seg_last = jnp.sum(
        (starts_row <= base + (tokens - 1.0)).astype(F32), axis=1, keepdims=True
    )
    first = lax.broadcasted_iota(jnp.int32, (tokens, tokens), 0)
    second = lax.broadcasted_iota(jnp.int32, (tokens, tokens), 1)
    same = seg_col == seg_row
    mask = jnp.where((first > second) & same, 1.0, 0.0)
    maskt = jnp.where((second > first) & same, 1.0, 0.0)
    mask_s[...] = rows(mask, mask)
    maskt_s[...] = rows(maskt, maskt)
    carried_s[...] = jnp.broadcast_to((seg_col == seg_prev).astype(F32), (tokens, LANES))
    keep_s[...] = jnp.broadcast_to((seg_col == seg_last).astype(F32), (tokens, LANES))
    flag_s[...] = jnp.broadcast_to((seg_last == seg_prev).astype(F32), (8, LANES))

    lane = lax.broadcasted_iota(jnp.int32, (1, LANES), 1)
    in_a = lane < HS
    mask_a = in_a.astype(F32).astype(BF16)
    mask_b = (1.0 - in_a.astype(F32)).astype(BF16)
    lower = jnp.where(first >= second, 1.0, 0.0).astype(BF16)
    upper = jnp.where(first <= second, 1.0, 0.0).astype(BF16)
    lower3 = lanes(lower, lower, lower)
    upper3 = lanes(upper, upper, upper)
    head_i = lax.broadcasted_iota(jnp.int32, (LANES, LANES), 0) // HS
    head_j = lax.broadcasted_iota(jnp.int32, (LANES, LANES), 1) // HS
    ones = jnp.where(head_i == head_j, 1.0, 0.0).astype(BF16)
    ones2 = rows(ones, ones)
    ones3 = rows(ones, ones, ones)

    def stacked(x):
        return rows(x * mask_a, x * mask_b)

    def pick(x):
        m = x.shape[0] // 2
        return jnp.where(in_a, x[:m], x[m:])

    def where_of(p):
        cols = pl.ds(pl.multiple_of(p * LANES, LANES), LANES)
        per = piece // LANES
        sub = pl.ds(pl.multiple_of(lax.rem(p, per) * LANES, LANES), LANES)
        return cols, p // per, sub

    def summarise(p):
        cols, slot, sub = where_of(p)
        r, k = r_ref[:, cols].astype(F32), k_ref[:, cols].astype(F32)
        v, dy = v_ref[:, cols], dy_ref[:, cols]
        lw = -jnp.exp(x_ref[:, cols])
        cum = dot(lower3, rows(*split3(lw)))
        lw_s[:, cols] = lw
        cum_s[:, cols] = cum
        last = cum[tokens - 1 : tokens]
        ending = k * jnp.exp(last - cum) * keep_s[...]
        reached = r * jnp.exp(cum - lw) * carried_s[...]
        vt, dyt = v.T, dy.T
        ends = pick(dot(lanes(vt, vt), rows(*split2(ending))))
        pulls = pick(dot(lanes(dyt, dyt), rows(*split2(reached))))
        dyv = dot(lanes(*split2(dy.astype(F32) * v.astype(F32))), ones2)
        dyv_s[:, cols] = dyv
        du = jnp.sum(dyv * r * k, axis=0, keepdims=True)
        through = jnp.exp(last) * flag_s[0:1]
        tail = rows(through, du, jnp.zeros((6, LANES), F32))
        for h in range(2):
            blk[h, slot, 0:HALF, sub] = ends[h * HALF : (h + 1) * HALF]
            blk[h, slot, HALF : 2 * HALF, sub] = pulls[h * HALF : (h + 1) * HALF]
            blk[h, slot, 2 * HALF : BLOCK_ROWS, sub] = tail

    def local_part(p):
        cols, _, _ = where_of(p)
        r, k = r_ref[:, cols].astype(F32), k_ref[:, cols].astype(F32)
        v, dy = v_ref[:, cols], dy_ref[:, cols]
        lw, cum = lw_s[:, cols], cum_s[:, cols]
        qh, ql = split2(r * jnp.exp(cum - lw))
        kh, kl = split2(k * jnp.exp(-cum))
        kh2, kl2 = stacked(kh), stacked(kl)
        at = dot_nt(lanes(kh2, kl2, kh2), lanes(qh, qh, ql))
        at = jnp.where(maskt_s[...] > 0.0, at, 0.0)
        da = jnp.where(mask_s[...] > 0.0, dot_nt(stacked(dy), v), 0.0)
        dat = jnp.where(maskt_s[...] > 0.0, dot_nt(stacked(v), dy), 0.0)
        dvv_s[:, cols] = pick(dot(lanes(*split2(at)), rows(dy, dy)))
        dah, dal = split2(da)
        dq_s[:, cols] = pick(dot(lanes(dah, dal, dah), rows(kh, kh, kl)))
        dth, dtl = split2(dat)
        dkk_s[:, cols] = pick(dot(lanes(dth, dtl, dth), rows(qh, qh, ql)))

    def finish(p):
        cols, slot, sub = where_of(p)
        r, k = r_ref[:, cols].astype(F32), k_ref[:, cols].astype(F32)
        v, dy = v_ref[:, cols], dy_ref[:, cols]
        u = u_ref[:, cols]
        lw, cum, dyv = lw_s[:, cols], cum_s[:, cols], dyv_s[:, cols]
        s = rows(fin[0, slot, 0:HALF, sub], fin[1, slot, 0:HALF, sub])
        g = rows(fin[0, slot, HALF : 2 * HALF, sub], fin[1, slot, HALF : 2 * HALF, sub])
        sh, sl = split2(rows(jnp.where(in_a, s, 0.0), jnp.where(in_a, 0.0, s)))
        gh, gl = split2(rows(jnp.where(in_a, g, 0.0), jnp.where(in_a, 0.0, g)))
        dq = dq_s[:, cols] + dot(lanes(dy, dy), rows(sh, sl)) * carried_s[...]
        de = dot(lanes(v, v), rows(gh, gl))
        last = cum[tokens - 1 : tokens]
        fade = jnp.exp(last - cum) * keep_s[...]
        ending = k * fade
        eh, el = split2(ending)
        eb, enc = jnp.exp(cum - lw), jnp.exp(-cum)
        bonus = dot(lanes(*split3(r * u * k)), ones3)
        dkk = dkk_s[:, cols]
        dv = dvv_s[:, cols] + dot_nt(lanes(eh, el, eh), lanes(gh, gh, gl))
        dv = dv + bonus * dy.astype(F32)
        du = dyv * u
        dr_ref[:, cols] = (dq * eb + du * k).astype(BF16)
        dk_ref[:, cols] = (dkk * enc + de * fade + du * r).astype(BF16)
        dv_ref[:, cols] = dv.astype(BF16)
        db = dq * (r * eb)
        ee = de * ending
        through = jnp.exp(last) * flag_s[0:1]
        tail = jnp.sum(ee, axis=0, keepdims=True)
        tail = tail + through * jnp.sum(s * g, axis=0, keepdims=True)
        total = db - dkk * (k * enc) - ee
        rev = dot(upper3, rows(*split3(total))) + tail - db
        dx_ref[:, cols] = (rev * lw).astype(BF16)
        du_ref[:, cols] = fin[0, slot, 2 * HALF + 1 : 2 * HALF + 2, sub]

    per = piece // LANES

    def run(part, low, count):
        if count % 2:
            for i in range(count):
                part(low + i)
            return

        def step(i, carry):
            part(low + 2 * i)
            part(low + 2 * i + 1)
            return carry

        lax.fori_loop(0, count // 2, step, 0)

    cuts = [pairs * c // 16 for c in (0, 2, 6, 10, 14, 16)]

    def remote(src, dst, send, recv, device):
        return pltpu.make_async_remote_copy(
            src_ref=src,
            dst_ref=dst,
            send_sem=send,
            recv_sem=recv,
            device_id=(device,),
            device_id_type=MESH,
        )

    late = core == 1
    e_rows, p_rows = slice(0, HALF), slice(HALF, 2 * HALF)
    t_row, u_row = slice(2 * HALF, 2 * HALF + 1), slice(2 * HALF + 1, 2 * HALF + 2)
    end_rows = slice(2 * HALF, BLOCK_ROWS)

    def tail_of(t, u):
        return rows(t, u, jnp.zeros((6, piece), F32))

    def combine(c, out):
        ta, tb = blk[core, c, t_row], rx1[c, t_row]
        ea, eb = blk[core, c, e_rows], rx1[c, e_rows]
        pa, pb = blk[core, c, p_rows], rx1[c, p_rows]
        out[c, e_rows] = jnp.where(late, ta * eb + ea, tb * ea + eb)
        out[c, p_rows] = jnp.where(late, pb + tb * pa, pa + ta * pb)
        out[c, end_rows] = tail_of(ta * tb, blk[core, c, u_row] + rx1[c, u_row])

    copies1, copies2 = [], []

    def pass_on(o):
        copies1[o - 1].wait_recv()
        target, device = at_chip(o)
        if o == chips:
            combine(chip, rx2)
            return
        combine(target, tx2)
        copies2.append(
            remote(tx2.at[target], rx2.at[chip], send2.at[o], recv2.at[o], device)
        )
        copies2[-1].start()

    for o in range(1, chips + 1):
        target, _ = at_chip(o)
        for load in loads[o - 1]:
            load.wait()
        run(summarise, target * per, per)
        if o == 1:
            pl.semaphore_wait(barrier, len(friends))
        copies1.append(
            remote(
                blk.at[1 - core, target],
                rx1.at[target],
                core_send.at[o - 1],
                core_recv.at[o - 1],
                partner,
            )
        )
        copies1[-1].start()
        if o > 1:
            pass_on(o - 1)
    run(local_part, cuts[0], cuts[1] - cuts[0])
    pass_on(chips)
    run(local_part, cuts[1], cuts[2] - cuts[1])
    for copy in copies2:
        copy.wait_recv()

    def forward(c, carry):
        f, t, du = carry
        tx4[c, e_rows] = f
        tc = rx2[c, t_row]
        tx4[c, t_row] = t
        return tc * f + rx2[c, e_rows], t * tc, du + rx2[c, u_row]

    zero, row = jnp.zeros((HALF, piece), F32), jnp.zeros((1, piece), F32)
    f, t, du = lax.fori_loop(0, chips, forward, (zero, row + 1.0, row))

    def backward(i, carry):
        c = chips - 1 - i
        b, t = carry
        tx4[c, p_rows] = b
        tc = rx2[c, t_row]
        tx4[c, u_row] = t
        return rx2[c, p_rows] + tc * b, t * tc

    b, t = lax.fori_loop(0, chips, backward, (zero, row + 1.0))
    tot[e_rows] = f
    tot[p_rows] = b
    tot[end_rows] = tail_of(t, du)

    ahead = remote(tot.at[e_rows], rx3f, send3.at[0], recv3.at[0], at_group(1))
    behind = remote(
        tot.at[p_rows], rx3b, send3.at[1], recv3.at[1], at_group(GROUPS - 1)
    )
    has_next, has_prev = group < GROUPS - 1, group > 0

    @pl.when(has_next)
    def _():
        ahead.start()

    @pl.when(has_prev)
    def _():
        behind.start()

    copies3 = []
    for o in range(1, GROUPS):
        copies3.append(
            remote(
                tot.at[end_rows],
                rx3t.at[o - 1],
                send3t.at[o - 1],
                recv3t.at[o - 1],
                at_group(o),
            )
        )
        copies3[-1].start()
    run(local_part, cuts[2], cuts[3] - cuts[2])

    @pl.when(has_prev)
    def _():
        ahead.wait_recv()

    @pl.when(jnp.logical_not(has_prev))
    def _():
        rx3f[...] = zero

    @pl.when(has_next)
    def _():
        behind.wait_recv()

    @pl.when(jnp.logical_not(has_next))
    def _():
        rx3b[...] = zero

    for copy in copies3:
        copy.wait_recv()
    du = tot[u_row]
    for o in range(1, GROUPS):
        du = du + rx3t[o - 1, 1:2]

    def carry_in(c, carry):
        tx4[c, e_rows] = tx4[c, e_rows] + tx4[c, t_row] * rx3f[...]
        tx4[c, p_rows] = tx4[c, p_rows] + tx4[c, u_row] * rx3b[...]
        tx4[c, end_rows] = tail_of(row, du)
        return carry

    lax.fori_loop(0, chips, carry_in, 0)

    copies4 = []
    for o in range(1, chips):
        target, device = at_chip(o)
        copies4.append(
            remote(tx4.at[target], rx4.at[chip], send4.at[o], recv4.at[o], device)
        )
        copies4[-1].start()
    rx4[chip] = tx4[chip]

    copies5 = []

    def share(o):
        c = lax.rem(chip - o + chips, chips)
        if o:
            copies4[o - 1].wait_recv()
        ta, tb = blk[core, c, t_row], rx1[c, t_row]
        ea, eb = blk[core, c, e_rows], rx1[c, e_rows]
        pa, pb = blk[core, c, p_rows], rx1[c, p_rows]
        fc, bc, end = rx4[c, e_rows], rx4[c, p_rows], rx4[c, end_rows]
        tx5[c, e_rows] = jnp.where(late, fc, ta * fc + ea)
        tx5[c, p_rows] = jnp.where(late, pa + ta * bc, bc)
        tx5[c, end_rows] = end
        copies5.append(
            remote(
                tx5.at[c],
                fin.at[core, c],
                core_send.at[chips + o],
                core_recv.at[chips + o],
                partner,
            )
        )
        copies5[-1].start()
        fin[core, c, e_rows] = jnp.where(late, tb * fc + eb, fc)
        fin[core, c, p_rows] = jnp.where(late, bc, pb + tb * bc)
        fin[core, c, end_rows] = end

    share(0)
    run(local_part, cuts[3], cuts[4] - cuts[3])
    share(1)
    run(local_part, cuts[4], cuts[5] - cuts[4])
    load_u.wait()
    results = (
        (dr_ref, dr_hbm),
        (dk_ref, dk_hbm),
        (dv_ref, dv_hbm),
        (dx_ref, dx_hbm),
        (du_ref, du_hbm),
    )
    stores = []
    for o in range(chips):
        if o + 2 < chips:
            share(o + 2)
        copies5[o].wait_recv()
        target = lax.rem(chip - o + chips, chips)
        run(finish, target * per, per)
        cols = pl.ds(pl.multiple_of(target * piece, LANES), piece)
        for i, (src, dst) in enumerate(results):
            stores.append(
                pltpu.make_async_copy(
                    src.at[:, cols], dst.at[:, cols], out_sem.at[i * chips + o]
                )
            )
            stores[-1].start()
    for store in stores:
        store.wait()

    for copy in copies1 + copies2 + copies3 + copies4 + copies5:
        copy.wait_send()

    @pl.when(has_next)
    def _():
        ahead.wait_send()

    @pl.when(has_prev)
    def _():
        behind.wait_send()


def hand_over(*refs):
    sem = refs[-1]
    count = len(refs) // 2
    copies = [
        pltpu.make_async_copy(refs[i], refs[count + i], sem.at[i]) for i in range(count)
    ]
    for copy in copies:
        copy.start()
    for copy in copies:
        copy.wait()


def body(
    n,
    acceptance_gate,
    lookup_matrix,
    payload_matrix,
    fading_parameter,
    present_reward,
    emitted_cotangent,
    paper_spans,
):
    tokens, width = acceptance_gate.shape
    chips = n // GROUPS // 2
    piece = width // chips
    full = pltpu.VMEM((tokens, width), F32)
    given = pltpu.VMEM((tokens, width), BF16)
    table = pltpu.VMEM((tokens, LANES), F32)
    table2 = pltpu.VMEM((2 * tokens, LANES), F32)
    half = pltpu.VMEM((chips, BLOCK_ROWS, piece), F32)
    both = pltpu.VMEM((2, chips, BLOCK_ROWS, piece), F32)
    state = pltpu.VMEM((HALF, piece), F32)
    sems = pltpu.SemaphoreType.DMA
    grad = jax.ShapeDtypeStruct((tokens, width), BF16)
    outs = pl.pallas_call(
        functools.partial(kernel, n),
        out_shape=(grad, grad, grad, grad, jax.ShapeDtypeStruct((1, width), F32)),
        in_specs=[pl.BlockSpec(memory_space=pltpu.HBM)] * 7,
        out_specs=[pl.BlockSpec(memory_space=pltpu.HBM)] * 5,
        scratch_shapes=[given] * 4
        + [pltpu.VMEM((1, width), F32)]
        + [given, given, given, full]
        + [pltpu.VMEM((1, width), F32), given]
        + [pltpu.VMEM((1, paper_spans.shape[0]), jnp.int32)]
        + [full] * 6
        + [table2, table2, table, table, pltpu.VMEM((8, LANES), F32)]
        + [both, half, half, half, pltpu.VMEM((BLOCK_ROWS, piece), F32)]
        + [state, state, pltpu.VMEM((GROUPS - 1, 8, piece), F32)]
        + [half, half, half, both]
        + [sems((5 * chips,)), sems((5 * chips,)), sems((2,)), sems((2 * chips,)), sems((2 * chips,))]
        + [sems((chips,)), sems((chips,))]
        + [sems((2,)), sems((2,)), sems((GROUPS - 1,)), sems((GROUPS - 1,))]
        + [sems((chips,)), sems((chips,))],
        compiler_params=pltpu.CompilerParams(
            collective_id=0,
            has_side_effects=True,
            vmem_limit_bytes=VMEM_LIMIT,
        ),
    )(
        acceptance_gate,
        lookup_matrix,
        payload_matrix,
        fading_parameter,
        present_reward.reshape(1, width),
        emitted_cotangent,
        paper_spans.reshape(1, -1),
    )
    outs = pl.pallas_call(
        hand_over,
        out_shape=[jax.ShapeDtypeStruct(out.shape, out.dtype) for out in outs],
        in_specs=[pl.BlockSpec(memory_space=pltpu.HBM)] * 5,
        out_specs=[pl.BlockSpec(memory_space=pltpu.HBM)] * 5,
        scratch_shapes=[sems((5,))],
        compiler_params=pltpu.CompilerParams(vmem_limit_bytes=VMEM_LIMIT),
    )(*outs)
    return (*outs[:4], outs[4].reshape(width))


def solution(mesh):
    row = P("seq", None)
    return jax.shard_map(
        functools.partial(body, mesh.shape["seq"]),
        mesh=mesh,
        in_specs=(row, row, row, row, P(), row, P()),
        out_specs=(row, row, row, row, P()),
        check_vma=False,
    )
```

```python
import functools

import jax
import jax.numpy as jnp
from jax import lax
from jax.experimental import pallas as pl
from jax.experimental.pallas import tpu as pltpu
from jax.sharding import PartitionSpec as P

HS = 64
LANES = 128
HALF = 32
BLOCK_ROWS = 72
GROUPS = 4
VMEM_LIMIT = 62 * 1024 * 1024
MESH = pl.DeviceIdType.MESH
F32 = jnp.float32
BF16 = jnp.bfloat16


def split2(x):
    hi = x.astype(BF16)
    lo = (x - hi.astype(F32)).astype(BF16)
    return hi, lo


def split3(x):
    hi = x.astype(BF16)
    rest = x - hi.astype(F32)
    mid = rest.astype(BF16)
    lo = (rest - mid.astype(F32)).astype(BF16)
    return hi, mid, lo


def lanes(*xs):
    return jnp.concatenate(xs, axis=1)


def rows(*xs):
    return jnp.concatenate(xs, axis=0)


def dot(a, b):
    return lax.dot_general(a, b, (((1,), (0,)), ((), ())), preferred_element_type=F32)


def dot_nt(a, b):
    return lax.dot_general(a, b, (((1,), (1,)), ((), ())), preferred_element_type=F32)


def kernel(
    n,
    r_hbm,
    k_hbm,
    v_hbm,
    x_hbm,
    u_hbm,
    dy_hbm,
    spans_hbm,
    dr_hbm,
    dk_hbm,
    dv_hbm,
    dx_hbm,
    du_hbm,
    dr_ref,
    dk_ref,
    dv_ref,
    dx_ref,
    du_ref,
    r_ref,
    k_ref,
    v_ref,
    x_ref,
    u_ref,
    dy_ref,
    spans_ref,
    lw_s,
    cum_s,
    dyv_s,
    dq_s,
    dkk_s,
    dvv_s,
    mask_s,
    maskt_s,
    carried_s,
    keep_s,
    flag_s,
    blk,
    rx1,
    tx2,
    rx2,
    tot,
    rx3f,
    rx3b,
    rx3t,
    tx4,
    rx4,
    tx5,
    fin,
    in_sem,
    out_sem,
    small_sem,
    core_send,
    core_recv,
    send2,
    recv2,
    send3,
    recv3,
    send3t,
    recv3t,
    send4,
    recv4,
):
    tokens, width = r_ref.shape
    pairs = width // LANES
    group_size = n // GROUPS
    chips = group_size // 2
    piece = width // chips
    me = lax.axis_index("seq")
    core = lax.rem(me, 2)
    chip = lax.rem(me // 2, chips)
    group = me // group_size
    partner = me + 1 - 2 * core

    def at_chip(offset):
        target = lax.rem(chip + offset, chips)
        return target, group * group_size + target * 2 + core

    def at_group(offset):
        return lax.rem(group + offset, GROUPS) * group_size + chip * 2 + core

    barrier = pltpu.get_barrier_semaphore()
    friends = [partner]
    friends += [at_chip(o)[1] for o in range(1, chips)]
    friends += [at_group(o) for o in range(1, GROUPS)]
    for friend in friends:
        pl.semaphore_signal(barrier, inc=1, device_id=(friend,), device_id_type=MESH)

    load_spans = pltpu.make_async_copy(spans_hbm, spans_ref, small_sem.at[0])
    load_u = pltpu.make_async_copy(u_hbm, u_ref, small_sem.at[1])
    load_spans.start()
    load_u.start()
    large = (
        (x_hbm, x_ref),
        (k_hbm, k_ref),
        (r_hbm, r_ref),
        (v_hbm, v_ref),
        (dy_hbm, dy_ref),
    )
    loads = []
    for o in range(1, chips + 1):
        target = lax.rem(chip + o, chips)
        cols = pl.ds(pl.multiple_of(target * piece, LANES), piece)
        loads.append(
            [
                pltpu.make_async_copy(
                    src.at[:, cols], dst.at[:, cols], in_sem.at[i * chips + o - 1]
                )
                for i, (src, dst) in enumerate(large)
            ]
        )
        for load in loads[-1]:
            load.start()

    load_spans.wait()
    docs = spans_ref.shape[1]
    spans_row = spans_ref[...].astype(F32)
    one = lax.broadcasted_iota(jnp.int32, (docs, docs), 0)
    two = lax.broadcasted_iota(jnp.int32, (docs, docs), 1)
    spread = jnp.broadcast_to(spans_row, (docs, docs))
    spans_col = jnp.sum(jnp.where(one == two, spread, 0.0), axis=1, keepdims=True)
    starts_col = jnp.sum(jnp.where(two < one, spread, 0.0), axis=1, keepdims=True)
    starts_row = jnp.sum(jnp.where(one < two, spans_col, 0.0), axis=0, keepdims=True)
    base = (me * tokens).astype(F32)
    pos_col = base + lax.broadcasted_iota(jnp.int32, (tokens, 1), 0).astype(F32)
    pos_row = base + lax.broadcasted_iota(jnp.int32, (1, tokens), 1).astype(F32)
    seg_col = jnp.sum((starts_row <= pos_col).astype(F32), axis=1, keepdims=True)
    seg_row = jnp.sum((starts_col <= pos_row).astype(F32), axis=0, keepdims=True)
    seg_prev = jnp.sum((starts_row <= base - 1.0).astype(F32), axis=1, keepdims=True)
    seg_last = jnp.sum(
        (starts_row <= base + (tokens - 1.0)).astype(F32), axis=1, keepdims=True
    )
    first = lax.broadcasted_iota(jnp.int32, (tokens, tokens), 0)
    second = lax.broadcasted_iota(jnp.int32, (tokens, tokens), 1)
    same = seg_col == seg_row
    mask = jnp.where((first > second) & same, 1.0, 0.0)
    maskt = jnp.where((second > first) & same, 1.0, 0.0)
    mask_s[...] = rows(mask, mask)
    maskt_s[...] = rows(maskt, maskt)
    carried_s[...] = jnp.broadcast_to((seg_col == seg_prev).astype(F32), (tokens, LANES))
    keep_s[...] = jnp.broadcast_to((seg_col == seg_last).astype(F32), (tokens, LANES))
    flag_s[...] = jnp.broadcast_to((seg_last == seg_prev).astype(F32), (8, LANES))

    lane = lax.broadcasted_iota(jnp.int32, (1, LANES), 1)
    in_a = lane < HS
    mask_a = in_a.astype(F32).astype(BF16)
    mask_b = (1.0 - in_a.astype(F32)).astype(BF16)
    lower = jnp.where(first >= second, 1.0, 0.0).astype(BF16)
    upper = jnp.where(first <= second, 1.0, 0.0).astype(BF16)
    lower3 = lanes(lower, lower, lower)
    upper2 = lanes(upper, upper)
    head_i = lax.broadcasted_iota(jnp.int32, (LANES, LANES), 0) // HS
    head_j = lax.broadcasted_iota(jnp.int32, (LANES, LANES), 1) // HS
    ones = jnp.where(head_i == head_j, 1.0, 0.0).astype(BF16)
    ones2 = rows(ones, ones)

    def stacked(x):
        return rows(x * mask_a, x * mask_b)

    def pick(x):
        m = x.shape[0] // 2
        return jnp.where(in_a, x[:m], x[m:])

    def where_of(p):
        cols = pl.ds(pl.multiple_of(p * LANES, LANES), LANES)
        per = piece // LANES
        sub = pl.ds(pl.multiple_of(lax.rem(p, per) * LANES, LANES), LANES)
        return cols, p // per, sub

    def summarise(p):
        cols, slot, sub = where_of(p)
        r, k = r_ref[:, cols].astype(F32), k_ref[:, cols].astype(F32)
        v, dy = v_ref[:, cols], dy_ref[:, cols]
        lw = -jnp.exp(x_ref[:, cols])
        cum = dot(lower3, rows(*split3(lw)))
        lw_s[:, cols] = lw
        cum_s[:, cols] = cum
        last = cum[tokens - 1 : tokens]
        ending = k * jnp.exp(last - cum) * keep_s[...]
        reached = r * jnp.exp(cum - lw) * carried_s[...]
        vt, dyt = v.T, dy.T
        ends = pick(dot(lanes(vt, vt), rows(*split2(ending))))
        pulls = pick(dot(lanes(dyt, dyt), rows(*split2(reached))))
        dyv = dot(lanes(*split2(dy.astype(F32) * v.astype(F32))), ones2)
        dyv_s[:, cols] = dyv
        du = jnp.sum(dyv * r * k, axis=0, keepdims=True)
        through = jnp.exp(last) * flag_s[0:1]
        tail = rows(through, du, jnp.zeros((6, LANES), F32))
        for h in range(2):
            blk[h, slot, 0:HALF, sub] = ends[h * HALF : (h + 1) * HALF]
            blk[h, slot, HALF : 2 * HALF, sub] = pulls[h * HALF : (h + 1) * HALF]
            blk[h, slot, 2 * HALF : BLOCK_ROWS, sub] = tail

    def local_part(p):
        cols, _, _ = where_of(p)
        r, k = r_ref[:, cols].astype(F32), k_ref[:, cols].astype(F32)
        v, dy = v_ref[:, cols], dy_ref[:, cols]
        lw, cum = lw_s[:, cols], cum_s[:, cols]
        qh, ql = split2(r * jnp.exp(cum - lw))
        kh, kl = split2(k * jnp.exp(-cum))
        kh2, kl2 = stacked(kh), stacked(kl)
        at = dot_nt(lanes(kh2, kl2, kh2), lanes(qh, qh, ql))
        at = jnp.where(maskt_s[...] > 0.0, at, 0.0)
        da = jnp.where(mask_s[...] > 0.0, dot_nt(stacked(dy), v), 0.0)
        dat = jnp.where(maskt_s[...] > 0.0, dot_nt(stacked(v), dy), 0.0)
        dvv_s[:, cols] = pick(dot(lanes(*split2(at)), rows(dy, dy)))
        dah, dal = split2(da)
        dq_s[:, cols] = pick(dot(lanes(dah, dal, dah), rows(kh, kh, kl)))
        dth, dtl = split2(dat)
        dkk_s[:, cols] = pick(dot(lanes(dth, dtl, dth), rows(qh, qh, ql)))

    def finish(p):
        cols, slot, sub = where_of(p)
        r, k = r_ref[:, cols].astype(F32), k_ref[:, cols].astype(F32)
        v, dy = v_ref[:, cols], dy_ref[:, cols]
        u = u_ref[:, cols]
        lw, cum, dyv = lw_s[:, cols], cum_s[:, cols], dyv_s[:, cols]
        s = rows(fin[0, slot, 0:HALF, sub], fin[1, slot, 0:HALF, sub])
        g = rows(fin[0, slot, HALF : 2 * HALF, sub], fin[1, slot, HALF : 2 * HALF, sub])
        sh, sl = split2(rows(jnp.where(in_a, s, 0.0), jnp.where(in_a, 0.0, s)))
        gh, gl = split2(rows(jnp.where(in_a, g, 0.0), jnp.where(in_a, 0.0, g)))
        dq = dq_s[:, cols] + dot(lanes(dy, dy), rows(sh, sl)) * carried_s[...]
        de = dot(lanes(v, v), rows(gh, gl))
        last = cum[tokens - 1 : tokens]
        fade = jnp.exp(last - cum) * keep_s[...]
        ending = k * fade
        eh, el = split2(ending)
        eb, enc = jnp.exp(cum - lw), jnp.exp(-cum)
        bonus = dot(lanes(*split2(r * u * k)), ones2)
        dkk = dkk_s[:, cols]
        dv = dvv_s[:, cols] + dot_nt(lanes(eh, el, eh), lanes(gh, gh, gl))
        dv = dv + bonus * dy.astype(F32)
        du = dyv * u
        dr_ref[:, cols] = (dq * eb + du * k).astype(BF16)
        dk_ref[:, cols] = (dkk * enc + de * fade + du * r).astype(BF16)
        dv_ref[:, cols] = dv.astype(BF16)
        db = dq * (r * eb)
        ee = de * ending
        through = jnp.exp(last) * flag_s[0:1]
        tail = jnp.sum(ee, axis=0, keepdims=True)
        tail = tail + through * jnp.sum(s * g, axis=0, keepdims=True)
        total = db - dkk * (k * enc) - ee
        rev = dot(upper2, rows(*split2(total))) + tail - db
        dx_ref[:, cols] = (rev * lw).astype(BF16)
        du_ref[:, cols] = fin[0, slot, 2 * HALF + 1 : 2 * HALF + 2, sub]

    per = piece // LANES

    def run(part, low, count, width=2):
        if count % width:
            width = 1

        def step(i, carry):
            for j in range(width):
                part(low + width * i + j)
            return carry

        lax.fori_loop(0, count // width, step, 0)

    cuts = [pairs * c // 16 for c in (0, 2, 6, 10, 14, 16)]

    def remote(src, dst, send, recv, device):
        return pltpu.make_async_remote_copy(
            src_ref=src,
            dst_ref=dst,
            send_sem=send,
            recv_sem=recv,
            device_id=(device,),
            device_id_type=MESH,
        )

    late = core == 1
    e_rows, p_rows = slice(0, HALF), slice(HALF, 2 * HALF)
    t_row, u_row = slice(2 * HALF, 2 * HALF + 1), slice(2 * HALF + 1, 2 * HALF + 2)
    end_rows = slice(2 * HALF, BLOCK_ROWS)

    def tail_of(t, u):
        return rows(t, u, jnp.zeros((6, piece), F32))

    def combine(c, out):
        ta, tb = blk[core, c, t_row], rx1[c, t_row]
        ea, eb = blk[core, c, e_rows], rx1[c, e_rows]
        pa, pb = blk[core, c, p_rows], rx1[c, p_rows]
        out[c, e_rows] = jnp.where(late, ta * eb + ea, tb * ea + eb)
        out[c, p_rows] = jnp.where(late, pb + tb * pa, pa + ta * pb)
        out[c, end_rows] = tail_of(ta * tb, blk[core, c, u_row] + rx1[c, u_row])

    copies1, copies2 = [], []

    def pass_on(o):
        copies1[o - 1].wait_recv()
        target, device = at_chip(o)
        if o == chips:
            combine(chip, rx2)
            return
        combine(target, tx2)
        copies2.append(
            remote(tx2.at[target], rx2.at[chip], send2.at[o], recv2.at[o], device)
        )
        copies2[-1].start()

    for o in range(1, chips + 1):
        target, _ = at_chip(o)
        for load in loads[o - 1]:
            load.wait()
        run(summarise, target * per, per, 4)
        if o == 1:
            pl.semaphore_wait(barrier, len(friends))
        copies1.append(
            remote(
                blk.at[1 - core, target],
                rx1.at[target],
                core_send.at[o - 1],
                core_recv.at[o - 1],
                partner,
            )
        )
        copies1[-1].start()
        if o > 1:
            pass_on(o - 1)
    run(local_part, cuts[0], cuts[1] - cuts[0])
    pass_on(chips)
    run(local_part, cuts[1], cuts[2] - cuts[1])
    for copy in copies2:
        copy.wait_recv()

    def forward(c, carry):
        f, t, du = carry
        tx4[c, e_rows] = f
        tc = rx2[c, t_row]
        tx4[c, t_row] = t
        return tc * f + rx2[c, e_rows], t * tc, du + rx2[c, u_row]

    zero, row = jnp.zeros((HALF, piece), F32), jnp.zeros((1, piece), F32)
    f, t, du = lax.fori_loop(0, chips, forward, (zero, row + 1.0, row))

    def backward(i, carry):
        c = chips - 1 - i
        b, t = carry
        tx4[c, p_rows] = b
        tc = rx2[c, t_row]
        tx4[c, u_row] = t
        return rx2[c, p_rows] + tc * b, t * tc

    b, t = lax.fori_loop(0, chips, backward, (zero, row + 1.0))
    tot[e_rows] = f
    tot[p_rows] = b
    tot[end_rows] = tail_of(t, du)

    ahead = remote(tot.at[e_rows], rx3f, send3.at[0], recv3.at[0], at_group(1))
    behind = remote(
        tot.at[p_rows], rx3b, send3.at[1], recv3.at[1], at_group(GROUPS - 1)
    )
    has_next, has_prev = group < GROUPS - 1, group > 0

    @pl.when(has_next)
    def _():
        ahead.start()

    @pl.when(has_prev)
    def _():
        behind.start()

    copies3 = []
    for o in range(1, GROUPS):
        copies3.append(
            remote(
                tot.at[end_rows],
                rx3t.at[o - 1],
                send3t.at[o - 1],
                recv3t.at[o - 1],
                at_group(o),
            )
        )
        copies3[-1].start()
    run(local_part, cuts[2], cuts[3] - cuts[2])

    @pl.when(has_prev)
    def _():
        ahead.wait_recv()

    @pl.when(jnp.logical_not(has_prev))
    def _():
        rx3f[...] = zero

    @pl.when(has_next)
    def _():
        behind.wait_recv()

    @pl.when(jnp.logical_not(has_next))
    def _():
        rx3b[...] = zero

    for copy in copies3:
        copy.wait_recv()
    du = tot[u_row]
    for o in range(1, GROUPS):
        du = du + rx3t[o - 1, 1:2]

    def carry_in(c, carry):
        tx4[c, e_rows] = tx4[c, e_rows] + tx4[c, t_row] * rx3f[...]
        tx4[c, p_rows] = tx4[c, p_rows] + tx4[c, u_row] * rx3b[...]
        tx4[c, end_rows] = tail_of(row, du)
        return carry

    lax.fori_loop(0, chips, carry_in, 0)

    copies4 = []
    for o in range(1, chips):
        target, device = at_chip(o)
        copies4.append(
            remote(tx4.at[target], rx4.at[chip], send4.at[o], recv4.at[o], device)
        )
        copies4[-1].start()
    rx4[chip] = tx4[chip]

    copies5 = []

    def share(o):
        c = lax.rem(chip - o + chips, chips)
        if o:
            copies4[o - 1].wait_recv()
        ta, tb = blk[core, c, t_row], rx1[c, t_row]
        ea, eb = blk[core, c, e_rows], rx1[c, e_rows]
        pa, pb = blk[core, c, p_rows], rx1[c, p_rows]
        fc, bc, end = rx4[c, e_rows], rx4[c, p_rows], rx4[c, end_rows]
        tx5[c, e_rows] = jnp.where(late, fc, ta * fc + ea)
        tx5[c, p_rows] = jnp.where(late, pa + ta * bc, bc)
        tx5[c, end_rows] = end
        copies5.append(
            remote(
                tx5.at[c],
                fin.at[core, c],
                core_send.at[chips + o],
                core_recv.at[chips + o],
                partner,
            )
        )
        copies5[-1].start()
        fin[core, c, e_rows] = jnp.where(late, tb * fc + eb, fc)
        fin[core, c, p_rows] = jnp.where(late, bc, pb + tb * bc)
        fin[core, c, end_rows] = end

    share(0)
    run(local_part, cuts[3], cuts[4] - cuts[3])
    share(1)
    run(local_part, cuts[4], cuts[5] - cuts[4])
    load_u.wait()
    results = (
        (dr_ref, dr_hbm),
        (dk_ref, dk_hbm),
        (dv_ref, dv_hbm),
        (dx_ref, dx_hbm),
        (du_ref, du_hbm),
    )
    stores = []
    for o in range(chips):
        if o + 2 < chips:
            share(o + 2)
        copies5[o].wait_recv()
        target = lax.rem(chip - o + chips, chips)
        run(finish, target * per, per, 4)
        cols = pl.ds(pl.multiple_of(target * piece, LANES), piece)
        for i, (src, dst) in enumerate(results):
            stores.append(
                pltpu.make_async_copy(
                    src.at[:, cols], dst.at[:, cols], out_sem.at[i * chips + o]
                )
            )
            stores[-1].start()
    for store in stores:
        store.wait()

    for copy in copies1 + copies2 + copies3 + copies4 + copies5:
        copy.wait_send()

    @pl.when(has_next)
    def _():
        ahead.wait_send()

    @pl.when(has_prev)
    def _():
        behind.wait_send()


def hand_over(*refs):
    count = len(refs) // 3
    sem = refs[-1]
    copies = [
        [
            pltpu.make_async_copy(refs[i], refs[2 * count + i], sem.at[i]),
            pltpu.make_async_copy(refs[2 * count + i], refs[count + i], sem.at[count + i]),
        ]
        for i in range(count)
    ]
    for load, _ in copies:
        load.start()
    for load, store in copies:
        load.wait()
        store.start()
    for _, store in copies:
        store.wait()


def body(
    n,
    acceptance_gate,
    lookup_matrix,
    payload_matrix,
    fading_parameter,
    present_reward,
    emitted_cotangent,
    paper_spans,
):
    tokens, width = acceptance_gate.shape
    chips = n // GROUPS // 2
    piece = width // chips
    full = pltpu.VMEM((tokens, width), F32)
    given = pltpu.VMEM((tokens, width), BF16)
    table = pltpu.VMEM((tokens, LANES), F32)
    table2 = pltpu.VMEM((2 * tokens, LANES), F32)
    half = pltpu.VMEM((chips, BLOCK_ROWS, piece), F32)
    both = pltpu.VMEM((2, chips, BLOCK_ROWS, piece), F32)
    state = pltpu.VMEM((HALF, piece), F32)
    sems = pltpu.SemaphoreType.DMA
    grad = jax.ShapeDtypeStruct((tokens, width), BF16)
    outs = pl.pallas_call(
        functools.partial(kernel, n),
        out_shape=(grad, grad, grad, grad, jax.ShapeDtypeStruct((1, width), F32)),
        in_specs=[pl.BlockSpec(memory_space=pltpu.HBM)] * 7,
        out_specs=[pl.BlockSpec(memory_space=pltpu.HBM)] * 5,
        scratch_shapes=[given] * 4
        + [pltpu.VMEM((1, width), F32)]
        + [given, given, given, full]
        + [pltpu.VMEM((1, width), F32), given]
        + [pltpu.VMEM((1, paper_spans.shape[0]), jnp.int32)]
        + [full] * 6
        + [table2, table2, table, table, pltpu.VMEM((8, LANES), F32)]
        + [both, half, half, half, pltpu.VMEM((BLOCK_ROWS, piece), F32)]
        + [state, state, pltpu.VMEM((GROUPS - 1, 8, piece), F32)]
        + [half, half, half, both]
        + [sems((5 * chips,)), sems((5 * chips,)), sems((2,)), sems((2 * chips,)), sems((2 * chips,))]
        + [sems((chips,)), sems((chips,))]
        + [sems((2,)), sems((2,)), sems((GROUPS - 1,)), sems((GROUPS - 1,))]
        + [sems((chips,)), sems((chips,))],
        compiler_params=pltpu.CompilerParams(
            collective_id=0,
            has_side_effects=True,
            vmem_limit_bytes=VMEM_LIMIT,
        ),
    )(
        acceptance_gate,
        lookup_matrix,
        payload_matrix,
        fading_parameter,
        present_reward.reshape(1, width),
        emitted_cotangent,
        paper_spans.reshape(1, -1),
    )
    outs = pl.pallas_call(
        hand_over,
        out_shape=[jax.ShapeDtypeStruct(out.shape, out.dtype) for out in outs],
        in_specs=[pl.BlockSpec(memory_space=pltpu.HBM)] * 5,
        out_specs=[pl.BlockSpec(memory_space=pltpu.HBM)] * 5,
        scratch_shapes=[pltpu.VMEM(out.shape, out.dtype) for out in outs] + [sems((10,))],
        compiler_params=pltpu.CompilerParams(vmem_limit_bytes=VMEM_LIMIT),
    )(*outs)
    return (*outs[:4], outs[4].reshape(width))


def solution(mesh):
    row = P("seq", None)
    return jax.shard_map(
        functools.partial(body, mesh.shape["seq"]),
        mesh=mesh,
        in_specs=(row, row, row, row, P(), row, P()),
        out_specs=(row, row, row, row, P()),
        check_vma=False,
    )
```

```python
import functools

import jax
import jax.numpy as jnp
from jax import lax
from jax.experimental import pallas as pl
from jax.experimental.pallas import tpu as pltpu
from jax.sharding import PartitionSpec as P

HS = 64
LANES = 128
HALF = 32
BLOCK_ROWS = 72
GROUPS = 4
VMEM_LIMIT = 62 * 1024 * 1024
MESH = pl.DeviceIdType.MESH
F32 = jnp.float32
BF16 = jnp.bfloat16


def split2(x):
    hi = x.astype(BF16)
    lo = (x - hi.astype(F32)).astype(BF16)
    return hi, lo


def split3(x):
    hi = x.astype(BF16)
    rest = x - hi.astype(F32)
    mid = rest.astype(BF16)
    lo = (rest - mid.astype(F32)).astype(BF16)
    return hi, mid, lo


def lanes(*xs):
    return jnp.concatenate(xs, axis=1)


def rows(*xs):
    return jnp.concatenate(xs, axis=0)


def dot(a, b):
    return lax.dot_general(a, b, (((1,), (0,)), ((), ())), preferred_element_type=F32)


def dot_nt(a, b):
    return lax.dot_general(a, b, (((1,), (1,)), ((), ())), preferred_element_type=F32)


def kernel(
    n,
    r_hbm,
    k_hbm,
    v_hbm,
    x_hbm,
    u_hbm,
    dy_hbm,
    spans_hbm,
    dr_hbm,
    dk_hbm,
    dv_hbm,
    dx_hbm,
    du_hbm,
    dr_ref,
    dk_ref,
    dv_ref,
    dx_ref,
    du_ref,
    r_ref,
    k_ref,
    v_ref,
    x_ref,
    u_ref,
    dy_ref,
    spans_ref,
    lw_s,
    cum_s,
    dyv_s,
    dq_s,
    dkk_s,
    dvv_s,
    mask_s,
    maskt_s,
    carried_s,
    keep_s,
    flag_s,
    blk,
    rx1,
    tx2,
    rx2,
    tot,
    rx3f,
    rx3b,
    rx3t,
    tx4,
    rx4,
    tx5,
    fin,
    in_sem,
    out_sem,
    small_sem,
    core_send,
    core_recv,
    send2,
    recv2,
    send3,
    recv3,
    send3t,
    recv3t,
    send4,
    recv4,
):
    tokens, width = r_ref.shape
    pairs = width // LANES
    group_size = n // GROUPS
    chips = group_size // 2
    piece = width // chips
    me = lax.axis_index("seq")
    core = lax.rem(me, 2)
    chip = lax.rem(me // 2, chips)
    group = me // group_size
    partner = me + 1 - 2 * core

    def at_chip(offset):
        target = lax.rem(chip + offset, chips)
        return target, group * group_size + target * 2 + core

    def at_group(offset):
        return lax.rem(group + offset, GROUPS) * group_size + chip * 2 + core

    barrier = pltpu.get_barrier_semaphore()
    friends = [partner]
    friends += [at_chip(o)[1] for o in range(1, chips)]
    friends += [at_group(o) for o in range(1, GROUPS)]
    for friend in friends:
        pl.semaphore_signal(barrier, inc=1, device_id=(friend,), device_id_type=MESH)

    load_spans = pltpu.make_async_copy(spans_hbm, spans_ref, small_sem.at[0])
    load_u = pltpu.make_async_copy(u_hbm, u_ref, small_sem.at[1])
    load_spans.start()
    load_u.start()
    large = (
        (x_hbm, x_ref),
        (k_hbm, k_ref),
        (r_hbm, r_ref),
        (v_hbm, v_ref),
        (dy_hbm, dy_ref),
    )
    loads = []
    for o in range(1, chips + 1):
        target = lax.rem(chip + o, chips)
        cols = pl.ds(pl.multiple_of(target * piece, LANES), piece)
        loads.append(
            [
                pltpu.make_async_copy(
                    src.at[:, cols], dst.at[:, cols], in_sem.at[i * chips + o - 1]
                )
                for i, (src, dst) in enumerate(large)
            ]
        )
        for load in loads[-1]:
            load.start()

    load_spans.wait()
    docs = spans_ref.shape[1]
    spans_row = spans_ref[...].astype(F32)
    one = lax.broadcasted_iota(jnp.int32, (docs, docs), 0)
    two = lax.broadcasted_iota(jnp.int32, (docs, docs), 1)
    spread = jnp.broadcast_to(spans_row, (docs, docs))
    spans_col = jnp.sum(jnp.where(one == two, spread, 0.0), axis=1, keepdims=True)
    starts_col = jnp.sum(jnp.where(two < one, spread, 0.0), axis=1, keepdims=True)
    starts_row = jnp.sum(jnp.where(one < two, spans_col, 0.0), axis=0, keepdims=True)
    base = (me * tokens).astype(F32)
    pos_col = base + lax.broadcasted_iota(jnp.int32, (tokens, 1), 0).astype(F32)
    pos_row = base + lax.broadcasted_iota(jnp.int32, (1, tokens), 1).astype(F32)
    seg_col = jnp.sum((starts_row <= pos_col).astype(F32), axis=1, keepdims=True)
    seg_row = jnp.sum((starts_col <= pos_row).astype(F32), axis=0, keepdims=True)
    seg_prev = jnp.sum((starts_row <= base - 1.0).astype(F32), axis=1, keepdims=True)
    seg_last = jnp.sum(
        (starts_row <= base + (tokens - 1.0)).astype(F32), axis=1, keepdims=True
    )
    first = lax.broadcasted_iota(jnp.int32, (tokens, tokens), 0)
    second = lax.broadcasted_iota(jnp.int32, (tokens, tokens), 1)
    same = seg_col == seg_row
    mask = jnp.where((first > second) & same, 1.0, 0.0)
    maskt = jnp.where((second > first) & same, 1.0, 0.0)
    mask_s[...] = rows(mask, mask)
    maskt_s[...] = rows(maskt, maskt)
    carried_s[...] = jnp.broadcast_to((seg_col == seg_prev).astype(F32), (tokens, LANES))
    keep_s[...] = jnp.broadcast_to((seg_col == seg_last).astype(F32), (tokens, LANES))
    flag_s[...] = jnp.broadcast_to((seg_last == seg_prev).astype(F32), (8, LANES))

    lane = lax.broadcasted_iota(jnp.int32, (1, LANES), 1)
    in_a = lane < HS
    mask_a = in_a.astype(F32).astype(BF16)
    mask_b = (1.0 - in_a.astype(F32)).astype(BF16)
    lower = jnp.where(first >= second, 1.0, 0.0).astype(BF16)
    upper = jnp.where(first <= second, 1.0, 0.0).astype(BF16)
    lower3 = lanes(lower, lower, lower)
    upper2 = lanes(upper, upper)
    head_i = lax.broadcasted_iota(jnp.int32, (LANES, LANES), 0) // HS
    head_j = lax.broadcasted_iota(jnp.int32, (LANES, LANES), 1) // HS
    ones = jnp.where(head_i == head_j, 1.0, 0.0).astype(BF16)
    ones2 = rows(ones, ones)

    def stacked(x):
        return rows(x * mask_a, x * mask_b)

    def pick(x):
        m = x.shape[0] // 2
        return jnp.where(in_a, x[:m], x[m:])

    def where_of(p):
        cols = pl.ds(pl.multiple_of(p * LANES, LANES), LANES)
        per = piece // LANES
        sub = pl.ds(pl.multiple_of(lax.rem(p, per) * LANES, LANES), LANES)
        return cols, p // per, sub

    def summarise(p):
        cols, slot, sub = where_of(p)
        r, k = r_ref[:, cols].astype(F32), k_ref[:, cols].astype(F32)
        v, dy = v_ref[:, cols], dy_ref[:, cols]
        lw = -jnp.exp(x_ref[:, cols])
        cum = dot(lower3, rows(*split3(lw)))
        lw_s[:, cols] = lw
        cum_s[:, cols] = cum
        last = cum[tokens - 1 : tokens]
        ending = k * jnp.exp(last - cum) * keep_s[...]
        reached = r * jnp.exp(cum - lw) * carried_s[...]
        vt, dyt = v.T, dy.T
        ends = pick(dot(lanes(vt, vt), rows(*split2(ending))))
        pulls = pick(dot(lanes(dyt, dyt), rows(*split2(reached))))
        dyv = dot(lanes(*split2(dy.astype(F32) * v.astype(F32))), ones2)
        dyv_s[:, cols] = dyv
        du = jnp.sum(dyv * r * k, axis=0, keepdims=True)
        through = jnp.exp(last) * flag_s[0:1]
        tail = rows(through, du, jnp.zeros((6, LANES), F32))
        for h in range(2):
            blk[h, slot, 0:HALF, sub] = ends[h * HALF : (h + 1) * HALF]
            blk[h, slot, HALF : 2 * HALF, sub] = pulls[h * HALF : (h + 1) * HALF]
            blk[h, slot, 2 * HALF : BLOCK_ROWS, sub] = tail

    def local_part(p):
        cols, _, _ = where_of(p)
        r, k = r_ref[:, cols].astype(F32), k_ref[:, cols].astype(F32)
        v, dy = v_ref[:, cols], dy_ref[:, cols]
        lw, cum = lw_s[:, cols], cum_s[:, cols]
        qh, ql = split2(r * jnp.exp(cum - lw))
        kh, kl = split2(k * jnp.exp(-cum))
        kh2, kl2 = stacked(kh), stacked(kl)
        at = dot_nt(lanes(kh2, kl2, kh2), lanes(qh, qh, ql))
        at = jnp.where(maskt_s[...] > 0.0, at, 0.0)
        da = jnp.where(mask_s[...] > 0.0, dot_nt(stacked(dy), v), 0.0)
        dat = jnp.where(maskt_s[...] > 0.0, dot_nt(stacked(v), dy), 0.0)
        dvv_s[:, cols] = pick(dot(lanes(*split2(at)), rows(dy, dy)))
        dah, dal = split2(da)
        dq_s[:, cols] = pick(dot(lanes(dah, dal, dah), rows(kh, kh, kl)))
        dth, dtl = split2(dat)
        dkk_s[:, cols] = pick(dot(lanes(dth, dtl, dth), rows(qh, qh, ql)))

    def finish(p):
        cols, slot, sub = where_of(p)
        r, k = r_ref[:, cols].astype(F32), k_ref[:, cols].astype(F32)
        v, dy = v_ref[:, cols], dy_ref[:, cols]
        u = u_ref[:, cols]
        lw, cum, dyv = lw_s[:, cols], cum_s[:, cols], dyv_s[:, cols]
        s = rows(fin[0, slot, 0:HALF, sub], fin[1, slot, 0:HALF, sub])
        g = rows(fin[0, slot, HALF : 2 * HALF, sub], fin[1, slot, HALF : 2 * HALF, sub])
        sh, sl = split2(rows(jnp.where(in_a, s, 0.0), jnp.where(in_a, 0.0, s)))
        gh, gl = split2(rows(jnp.where(in_a, g, 0.0), jnp.where(in_a, 0.0, g)))
        dq = dq_s[:, cols] + dot(lanes(dy, dy), rows(sh, sl)) * carried_s[...]
        de = dot(lanes(v, v), rows(gh, gl))
        last = cum[tokens - 1 : tokens]
        fade = jnp.exp(last - cum) * keep_s[...]
        ending = k * fade
        eh, el = split2(ending)
        eb, enc = jnp.exp(cum - lw), jnp.exp(-cum)
        bonus = dot(lanes(*split2(r * u * k)), ones2)
        dkk = dkk_s[:, cols]
        dv = dvv_s[:, cols] + dot_nt(lanes(eh, el, eh), lanes(gh, gh, gl))
        dv = dv + bonus * dy.astype(F32)
        du = dyv * u
        dr_ref[:, cols] = (dq * eb + du * k).astype(BF16)
        dk_ref[:, cols] = (dkk * enc + de * fade + du * r).astype(BF16)
        dv_ref[:, cols] = dv.astype(BF16)
        db = dq * (r * eb)
        ee = de * ending
        through = jnp.exp(last) * flag_s[0:1]
        tail = jnp.sum(ee, axis=0, keepdims=True)
        tail = tail + through * jnp.sum(s * g, axis=0, keepdims=True)
        total = db - dkk * (k * enc) - ee
        rev = dot(upper2, rows(*split2(total))) + tail - db
        dx_ref[:, cols] = (rev * lw).astype(BF16)
        du_ref[:, cols] = fin[0, slot, 2 * HALF + 1 : 2 * HALF + 2, sub]

    per = piece // LANES

    def run(part, low, count, width=4):
        while count % width:
            width //= 2

        def step(i, carry):
            for j in range(width):
                part(low + width * i + j)
            return carry

        lax.fori_loop(0, count // width, step, 0)

    cuts = [pairs * c // 16 for c in (0, 2, 6, 10, 14, 16)]

    def remote(src, dst, send, recv, device):
        return pltpu.make_async_remote_copy(
            src_ref=src,
            dst_ref=dst,
            send_sem=send,
            recv_sem=recv,
            device_id=(device,),
            device_id_type=MESH,
        )

    late = core == 1
    e_rows, p_rows = slice(0, HALF), slice(HALF, 2 * HALF)
    t_row, u_row = slice(2 * HALF, 2 * HALF + 1), slice(2 * HALF + 1, 2 * HALF + 2)
    end_rows = slice(2 * HALF, BLOCK_ROWS)

    def tail_of(t, u):
        return rows(t, u, jnp.zeros((6, piece), F32))

    def combine(c, out):
        ta, tb = blk[core, c, t_row], rx1[c, t_row]
        ea, eb = blk[core, c, e_rows], rx1[c, e_rows]
        pa, pb = blk[core, c, p_rows], rx1[c, p_rows]
        out[c, e_rows] = jnp.where(late, ta * eb + ea, tb * ea + eb)
        out[c, p_rows] = jnp.where(late, pb + tb * pa, pa + ta * pb)
        out[c, end_rows] = tail_of(ta * tb, blk[core, c, u_row] + rx1[c, u_row])

    copies1, copies2 = [], []

    def pass_on(o):
        copies1[o - 1].wait_recv()
        target, device = at_chip(o)
        if o == chips:
            combine(chip, rx2)
            return
        combine(target, tx2)
        copies2.append(
            remote(tx2.at[target], rx2.at[chip], send2.at[o], recv2.at[o], device)
        )
        copies2[-1].start()

    for o in range(1, chips + 1):
        target, _ = at_chip(o)
        for load in loads[o - 1]:
            load.wait()
        run(summarise, target * per, per, 4)
        if o == 1:
            pl.semaphore_wait(barrier, len(friends))
        copies1.append(
            remote(
                blk.at[1 - core, target],
                rx1.at[target],
                core_send.at[o - 1],
                core_recv.at[o - 1],
                partner,
            )
        )
        copies1[-1].start()
        if o > 1:
            pass_on(o - 1)
    run(local_part, cuts[0], cuts[1] - cuts[0])
    pass_on(chips)
    run(local_part, cuts[1], cuts[2] - cuts[1])
    for copy in copies2:
        copy.wait_recv()

    def forward(c, carry):
        f, t, du = carry
        tx4[c, e_rows] = f
        tc = rx2[c, t_row]
        tx4[c, t_row] = t
        return tc * f + rx2[c, e_rows], t * tc, du + rx2[c, u_row]

    zero, row = jnp.zeros((HALF, piece), F32), jnp.zeros((1, piece), F32)
    f, t, du = lax.fori_loop(0, chips, forward, (zero, row + 1.0, row))

    def backward(i, carry):
        c = chips - 1 - i
        b, t = carry
        tx4[c, p_rows] = b
        tc = rx2[c, t_row]
        tx4[c, u_row] = t
        return rx2[c, p_rows] + tc * b, t * tc

    b, t = lax.fori_loop(0, chips, backward, (zero, row + 1.0))
    tot[e_rows] = f
    tot[p_rows] = b
    tot[end_rows] = tail_of(t, du)

    ahead = remote(tot.at[e_rows], rx3f, send3.at[0], recv3.at[0], at_group(1))
    behind = remote(
        tot.at[p_rows], rx3b, send3.at[1], recv3.at[1], at_group(GROUPS - 1)
    )
    has_next, has_prev = group < GROUPS - 1, group > 0

    @pl.when(has_next)
    def _():
        ahead.start()

    @pl.when(has_prev)
    def _():
        behind.start()

    copies3 = []
    for o in range(1, GROUPS):
        copies3.append(
            remote(
                tot.at[end_rows],
                rx3t.at[o - 1],
                send3t.at[o - 1],
                recv3t.at[o - 1],
                at_group(o),
            )
        )
        copies3[-1].start()
    run(local_part, cuts[2], cuts[3] - cuts[2])

    @pl.when(has_prev)
    def _():
        ahead.wait_recv()

    @pl.when(jnp.logical_not(has_prev))
    def _():
        rx3f[...] = zero

    @pl.when(has_next)
    def _():
        behind.wait_recv()

    @pl.when(jnp.logical_not(has_next))
    def _():
        rx3b[...] = zero

    for copy in copies3:
        copy.wait_recv()
    du = tot[u_row]
    for o in range(1, GROUPS):
        du = du + rx3t[o - 1, 1:2]

    def carry_in(c, carry):
        tx4[c, e_rows] = tx4[c, e_rows] + tx4[c, t_row] * rx3f[...]
        tx4[c, p_rows] = tx4[c, p_rows] + tx4[c, u_row] * rx3b[...]
        tx4[c, end_rows] = tail_of(row, du)
        return carry

    lax.fori_loop(0, chips, carry_in, 0)

    copies4 = []
    for o in range(1, chips):
        target, device = at_chip(o)
        copies4.append(
            remote(tx4.at[target], rx4.at[chip], send4.at[o], recv4.at[o], device)
        )
        copies4[-1].start()
    rx4[chip] = tx4[chip]

    copies5 = []

    def share(o):
        c = lax.rem(chip - o + chips, chips)
        if o:
            copies4[o - 1].wait_recv()
        ta, tb = blk[core, c, t_row], rx1[c, t_row]
        ea, eb = blk[core, c, e_rows], rx1[c, e_rows]
        pa, pb = blk[core, c, p_rows], rx1[c, p_rows]
        fc, bc, end = rx4[c, e_rows], rx4[c, p_rows], rx4[c, end_rows]
        tx5[c, e_rows] = jnp.where(late, fc, ta * fc + ea)
        tx5[c, p_rows] = jnp.where(late, pa + ta * bc, bc)
        tx5[c, end_rows] = end
        copies5.append(
            remote(
                tx5.at[c],
                fin.at[core, c],
                core_send.at[chips + o],
                core_recv.at[chips + o],
                partner,
            )
        )
        copies5[-1].start()
        fin[core, c, e_rows] = jnp.where(late, tb * fc + eb, fc)
        fin[core, c, p_rows] = jnp.where(late, bc, pb + tb * bc)
        fin[core, c, end_rows] = end

    share(0)
    run(local_part, cuts[3], cuts[4] - cuts[3])
    share(1)
    run(local_part, cuts[4], cuts[5] - cuts[4])
    load_u.wait()
    results = (
        (dr_ref, dr_hbm),
        (dk_ref, dk_hbm),
        (dv_ref, dv_hbm),
        (dx_ref, dx_hbm),
        (du_ref, du_hbm),
    )
    stores = []
    for o in range(chips):
        if o + 2 < chips:
            share(o + 2)
        copies5[o].wait_recv()
        target = lax.rem(chip - o + chips, chips)
        run(finish, target * per, per, 4)
        cols = pl.ds(pl.multiple_of(target * piece, LANES), piece)
        for i, (src, dst) in enumerate(results):
            stores.append(
                pltpu.make_async_copy(
                    src.at[:, cols], dst.at[:, cols], out_sem.at[i * chips + o]
                )
            )
            stores[-1].start()
    for store in stores:
        store.wait()

    for copy in copies1 + copies2 + copies3 + copies4 + copies5:
        copy.wait_send()

    @pl.when(has_next)
    def _():
        ahead.wait_send()

    @pl.when(has_prev)
    def _():
        behind.wait_send()


def hand_over(*refs):
    count = len(refs) // 3
    sem = refs[-1]
    copies = [
        [
            pltpu.make_async_copy(refs[i], refs[2 * count + i], sem.at[i]),
            pltpu.make_async_copy(refs[2 * count + i], refs[count + i], sem.at[count + i]),
        ]
        for i in range(count)
    ]
    for load, _ in copies:
        load.start()
    for load, store in copies:
        load.wait()
        store.start()
    for _, store in copies:
        store.wait()


def body(
    n,
    acceptance_gate,
    lookup_matrix,
    payload_matrix,
    fading_parameter,
    present_reward,
    emitted_cotangent,
    paper_spans,
):
    tokens, width = acceptance_gate.shape
    chips = n // GROUPS // 2
    piece = width // chips
    full = pltpu.VMEM((tokens, width), F32)
    given = pltpu.VMEM((tokens, width), BF16)
    table = pltpu.VMEM((tokens, LANES), F32)
    table2 = pltpu.VMEM((2 * tokens, LANES), F32)
    half = pltpu.VMEM((chips, BLOCK_ROWS, piece), F32)
    both = pltpu.VMEM((2, chips, BLOCK_ROWS, piece), F32)
    state = pltpu.VMEM((HALF, piece), F32)
    sems = pltpu.SemaphoreType.DMA
    grad = jax.ShapeDtypeStruct((tokens, width), BF16)
    outs = pl.pallas_call(
        functools.partial(kernel, n),
        out_shape=(grad, grad, grad, grad, jax.ShapeDtypeStruct((1, width), F32)),
        in_specs=[pl.BlockSpec(memory_space=pltpu.HBM)] * 7,
        out_specs=[pl.BlockSpec(memory_space=pltpu.HBM)] * 5,
        scratch_shapes=[given] * 4
        + [pltpu.VMEM((1, width), F32)]
        + [given, given, given, full]
        + [pltpu.VMEM((1, width), F32), given]
        + [pltpu.VMEM((1, paper_spans.shape[0]), jnp.int32)]
        + [full] * 6
        + [table2, table2, table, table, pltpu.VMEM((8, LANES), F32)]
        + [both, half, half, half, pltpu.VMEM((BLOCK_ROWS, piece), F32)]
        + [state, state, pltpu.VMEM((GROUPS - 1, 8, piece), F32)]
        + [half, half, half, both]
        + [sems((5 * chips,)), sems((5 * chips,)), sems((2,)), sems((2 * chips,)), sems((2 * chips,))]
        + [sems((chips,)), sems((chips,))]
        + [sems((2,)), sems((2,)), sems((GROUPS - 1,)), sems((GROUPS - 1,))]
        + [sems((chips,)), sems((chips,))],
        compiler_params=pltpu.CompilerParams(
            collective_id=0,
            has_side_effects=True,
            vmem_limit_bytes=VMEM_LIMIT,
        ),
    )(
        acceptance_gate,
        lookup_matrix,
        payload_matrix,
        fading_parameter,
        present_reward.reshape(1, width),
        emitted_cotangent,
        paper_spans.reshape(1, -1),
    )
    outs = pl.pallas_call(
        hand_over,
        out_shape=[jax.ShapeDtypeStruct(out.shape, out.dtype) for out in outs],
        in_specs=[pl.BlockSpec(memory_space=pltpu.HBM)] * 5,
        out_specs=[pl.BlockSpec(memory_space=pltpu.HBM)] * 5,
        scratch_shapes=[pltpu.VMEM(out.shape, out.dtype) for out in outs] + [sems((10,))],
        compiler_params=pltpu.CompilerParams(vmem_limit_bytes=VMEM_LIMIT),
    )(*outs)
    return (*outs[:4], outs[4].reshape(width))


def solution(mesh):
    row = P("seq", None)
    return jax.shard_map(
        functools.partial(body, mesh.shape["seq"]),
        mesh=mesh,
        in_specs=(row, row, row, row, P(), row, P()),
        out_specs=(row, row, row, row, P()),
        check_vma=False,
    )
```
